128 devices in a mesh: tm: 2 (over core), tile: 64 (over z, y, x).
Axes of the slice: x: 4, y: 4, z: 4, core: 2. Of those that a mesh axis runs over, the one named last changes fastest.
Arguments:
- features: bfloat16 [1, 8, 256, 64, 192], P(None, 'tm', 'tile'), may hold values from -60 to 60
- gain_one: float32 [192], replicated, may hold values from 0.5 to 1.5
- shift_one: float32 [192], replicated, may hold values from -3 to 3
- kernel_one: bfloat16 [3, 3, 3, 192, 192], replicated, may hold values from -0.078125 to 0.078125
- bias_one: float32 [192], replicated, may hold values from -3 to 3
- gain_two: float32 [192], replicated, may hold values from 0.5 to 1.5
- shift_two: float32 [192], replicated, may hold values from -3 to 3
- kernel_two: bfloat16 [3, 3, 3, 192, 192], replicated, may hold values from -0.078125 to 0.078125
- bias_two: float32 [192], replicated, may hold values from -3 to 3
- up_kernel: bfloat16 [3, 3, 192, 96], replicated, may hold values from -0.15625 to 0.15625
- up_bias: float32 [96], replicated, may hold values from -3 to 3
Outputs:
- decoded: bfloat16 [1, 8, 512, 64, 192], P(None, 'tm', 'tile')
The draws below stay inside these ranges and needn't reach their ends.
All inputs are finite; a program needn't handle non-finite values.
Results may differ from the reference program's by a relative error of at most 0.009.
Values may be sent and summed in bfloat16 or wider, within the bound.
No kernel may reach another device: no remote copies, remote signals or barrier semaphores. Data moves between devices by JAX's collectives and lax.ppermute only.
A program may use at most 128 MiB of HBM per device.

```python
import jax
import jax.numpy as jnp
from jax import lax

C = 192
C2 = 96
G = 32
CLIPS = 1
W = 64
FRAMES = 8
H = 256


def draw_features(key, part):
    noise_key, row_key, col_key = jax.random.split(key, 3)
    shape_all = (CLIPS, FRAMES, H, W, C)
    row_place = jnp.arange(H, dtype=jnp.float32) / max(H - 1, 1)
    row_scale = 10.0 ** (jax.random.uniform(row_key, (H,), jnp.float32) - 0.5) * 3.0 ** (row_place - 1.0)
    col_scale = 10.0 ** (jax.random.uniform(col_key, (W,), jnp.float32) - 0.5)
    noise_draw = jax.random.truncated_normal(noise_key, -6.0, 6.0, shape_all, jnp.float32)
    scaled = noise_draw * row_scale[None, None, :, None, None] * col_scale[None, None, None, :, None]
    return scaled.astype(jnp.bfloat16)


def noise(rng, shape, width, most, held_as=jnp.bfloat16):
    drawn = width * jax.random.normal(rng, shape, jnp.float32)
    return jnp.clip(drawn, min=-most, max=most).astype(held_as)


def setup_inputs(seed: int = 0) -> dict:
    streams_of = jax.random.split(jax.random.key(seed), 12)
    features = draw_features(jax.random.fold_in(streams_of[11], 71), 0)
    gain_one = jnp.clip(1.0 + 0.1 * jax.random.normal(streams_of[1], (C,), jnp.float32), 0.5, 1.5)
    shift_one = noise(streams_of[2], (C,), 0.5, 3.0, jnp.float32)
    kernel_one = noise(streams_of[3], (3, 3, 3, C, C), (27 * C) ** -0.5, 0.078125)
    bias_one = noise(streams_of[4], (C,), 0.5, 3.0, jnp.float32)
    gain_two = jnp.clip(1.0 + 0.1 * jax.random.normal(streams_of[5], (C,), jnp.float32), 0.5, 1.5)
    shift_two = noise(streams_of[6], (C,), 0.5, 3.0, jnp.float32)
    kernel_two = noise(streams_of[7], (3, 3, 3, C, C), (27 * C) ** -0.5, 0.078125)
    bias_two = noise(streams_of[8], (C,), 0.5, 3.0, jnp.float32)
    up_kernel = noise(streams_of[9], (3, 3, C, C2), (9 * C) ** -0.5, 0.15625)
    up_bias = noise(streams_of[10], (C2,), 0.5, 3.0, jnp.float32)
    return {"features": features, "gain_one": gain_one, "shift_one": shift_one, "kernel_one": kernel_one, "bias_one": bias_one, "gain_two": gain_two, "shift_two": shift_two, "kernel_two": kernel_two, "bias_two": bias_two, "up_kernel": up_kernel, "up_bias": up_bias}


epsilon = 1e-06

def group_act(values_in, gain_vec, shift_vec):
    clip_count, frame_count, row_count, col_count, chan_count = values_in.shape
    grouped = values_in.reshape(clip_count, frame_count, row_count, col_count, G, chan_count // G)
    centre_value = lax.optimization_barrier(jnp.mean(grouped, axis=(2, 3, 5), keepdims=True))
    centered = grouped - centre_value
    spread_value = lax.optimization_barrier(jnp.mean(centered * centered, axis=(2, 3, 5), keepdims=True))
    normed = (centered * lax.rsqrt(spread_value + epsilon)).reshape(values_in.shape)
    return jax.nn.silu(normed * gain_vec + shift_vec).astype(jnp.bfloat16)

def causal_taps(padded, kernel, bias_term):
    clip_count, frame_span, row_span, col_count, chan_count = padded.shape
    out_frames = frame_span - 2
    out_rows = row_span - 2
    widened = jnp.pad(padded, ((0, 0), (0, 0), (0, 0), (1, 1), (0, 0)))
    accumulated = jnp.zeros((clip_count * out_frames * out_rows * col_count, kernel.shape[-1]), jnp.float32)
    for time_tap in range(3):
        for row_tap in range(3):
            slab_part = widened[:, time_tap:time_tap + out_frames, row_tap:row_tap + out_rows]
            stacked = jnp.concatenate([slab_part[:, :, :, col_tap:col_tap + col_count] for col_tap in range(3)], axis=-1)
            accumulated = accumulated + jnp.dot(stacked.reshape(-1, 3 * chan_count), kernel[time_tap, row_tap].reshape(3 * chan_count, -1), preferred_element_type=jnp.float32)
    return accumulated.reshape(clip_count, out_frames, out_rows, col_count, -1) + bias_term

def plane_taps(padded, kernel):
    clip_count, frame_count, row_span, col_span, chan_count = padded.shape
    out_rows = row_span - 2
    out_cols = col_span - 2
    accumulated = jnp.zeros((clip_count * frame_count * out_rows * out_cols, kernel.shape[-1]), jnp.float32)
    for row_tap in range(3):
        slab_part = padded[:, :, row_tap:row_tap + out_rows]
        stacked = jnp.concatenate([slab_part[:, :, :, col_tap:col_tap + out_cols] for col_tap in range(3)], axis=-1)
        accumulated = accumulated + jnp.dot(stacked.reshape(-1, 3 * chan_count), kernel[row_tap].reshape(3 * chan_count, -1), preferred_element_type=jnp.float32)
    return accumulated.reshape(clip_count, frame_count, out_rows, out_cols, -1)

def reference(features, gain_one, shift_one, kernel_one, bias_one, gain_two, shift_two, kernel_two, bias_two, up_kernel, up_bias):
    outputs = []
    for clip_index in range(CLIPS):
        source = features[clip_index:clip_index + 1].astype(jnp.float32)
        first_act = group_act(source, gain_one, shift_one)
        first_pad = jnp.pad(first_act, ((0, 0), (2, 0), (1, 1), (0, 0), (0, 0)))
        hidden = causal_taps(first_pad, kernel_one, bias_one).astype(jnp.bfloat16)
        second = group_act(hidden.astype(jnp.float32), gain_two, shift_two)
        second_pad = jnp.pad(second, ((0, 0), (2, 0), (1, 1), (0, 0), (0, 0)))
        joined = (source + causal_taps(second_pad, kernel_two, bias_two)).astype(jnp.bfloat16)
        doubled = jnp.repeat(jnp.repeat(joined, 2, axis=2), 2, axis=3)
        doubled_pad = jnp.pad(doubled, ((0, 0), (0, 0), (1, 1), (1, 1), (0, 0)))
        produced = (plane_taps(doubled_pad, up_kernel) + up_bias).astype(jnp.bfloat16)
        outputs.append(produced.reshape(1, FRAMES, 2 * H, W, 2 * C2))
    return jnp.concatenate(outputs, axis=0)
```

```python
import functools

import jax
import jax.numpy as jnp
from jax import lax
from jax.experimental import pallas as pl
from jax.experimental.pallas import tpu as pltpu
from jax.sharding import PartitionSpec as P

G = 32
EPS = 1e-06
F32 = jnp.float32
BF16 = jnp.bfloat16
VM = pl.BlockSpec(memory_space=pltpu.VMEM)


def dot32(a, b):
    return jnp.dot(a, b, precision=lax.Precision.HIGHEST, preferred_element_type=F32)


def spread(chan):
    lane = lax.broadcasted_iota(jnp.int32, (128, chan), 0)
    col = lax.broadcasted_iota(jnp.int32, (128, chan), 1)
    low = (lane % G) * (chan // G)
    return jnp.where((col >= low) & (col < low + chan // G), 1.0, 0.0).astype(F32)


def gather_groups(chan):
    lane = lax.broadcasted_iota(jnp.int32, (chan, 128), 1)
    col = lax.broadcasted_iota(jnp.int32, (chan, 128), 0)
    low = (lane % G) * (chan // G)
    return jnp.where((col >= low) & (col < low + chan // G), 1.0, 0.0).astype(F32)


def frame_mask(first):
    lane = lax.broadcasted_iota(jnp.int32, (8, 128), 1)
    row = lax.broadcasted_iota(jnp.int32, (8, 128), 0)
    low = (row - first) * G
    return (lane >= low) & (lane < low + G)


def stack_rows(rows):
    width = rows[0].shape[1]
    index = lax.broadcasted_iota(jnp.int32, (8, width), 0)
    out = jnp.zeros((8, width), F32)
    for i, r in enumerate(rows):
        out = jnp.where(index == i, jnp.broadcast_to(r, (8, width)), out)
    return out


def local_stats(load, frames, count, chan, stat_ref):
    mask = frame_mask(0)
    to_group, to_chan = gather_groups(chan), spread(chan)
    sums = stack_rows([jnp.sum(load(f), axis=0, keepdims=True) for f in range(frames)])
    mean = jnp.where(mask, dot32(sums, to_group), 0.0) / count
    mean_chan = dot32(mean, to_chan)
    squares = []
    for f in range(frames):
        d = load(f) - mean_chan[f : f + 1]
        squares.append(jnp.sum(d * d, axis=0, keepdims=True))
    square = jnp.where(mask, dot32(stack_rows(squares), to_group), 0.0)
    packed = jnp.concatenate(
        [jnp.sum(mean, axis=0, keepdims=True), jnp.sum(square, axis=0, keepdims=True)], axis=0
    )
    stat_ref[...] = jnp.broadcast_to(packed[None], stat_ref.shape)


def global_stats(stat_ref, mean_ref, scale_ref, gain_ref, count):
    tiles = stat_ref.shape[0] // 2
    chan = mean_ref.shape[-1]
    to_chan = spread(chan)
    means, spreads = [], []
    for half in range(2):
        part = stat_ref[half * tiles : (half + 1) * tiles]
        total = jnp.sum(part, axis=0)
        mean = total[0:1] / tiles
        off = part - mean[None]
        spread_sum = total[1:2] + count * jnp.sum(off * off, axis=0)[0:1]
        means.append(mean)
        spreads.append(spread_sum / (tiles * count))
    m0, m1 = frame_mask(0), frame_mask(4)
    mean8 = jnp.where(m0, means[0], 0.0) + jnp.where(m1, means[1], 0.0)
    inv8 = jnp.where(m0, lax.rsqrt(spreads[0] + EPS), 0.0) + jnp.where(
        m1, lax.rsqrt(spreads[1] + EPS), 0.0
    )
    mean_chan = dot32(mean8, to_chan)
    scale = dot32(inv8, to_chan) * gain_ref[...]
    for f in range(8):
        mean_ref[f] = mean_chan[f : f + 1]
        scale_ref[f] = scale[f : f + 1]


def shifted(v):
    rows = v.shape[0]
    index = lax.broadcasted_iota(jnp.int32, v.shape, 0)
    left = jnp.where(index == 0, 0.0, pltpu.roll(v, 1, axis=0))
    right = jnp.where(index == rows - 1, 0.0, pltpu.roll(v, rows - 1, axis=0))
    return left, right


def put_row(v, s_ref, t_ref, f, r, out_rows, back):
    a, b = v[:, :128], v[:, 128:192]
    a_left, a_right = shifted(a)
    b_left, b_right = shifted(b)
    s_ref[f, r, :, 0:128] = a_left.astype(BF16)
    s_ref[f, r, :, 128:256] = a.astype(BF16)
    s_ref[f, r, :, 256:384] = a_right.astype(BF16)
    s_ref[f, r, :, 384:512] = jnp.concatenate([b_left, b], axis=1).astype(BF16)
    tail = b_right.astype(BF16)
    for k in range(back):
        if 0 <= r - k < out_rows:
            t_ref[f, r - k, :, 64 * k : 64 * k + 64] = tail


def silu(u):
    half = 0.5 * u
    return half + half * jnp.tanh(half)


def tap_weights(w_ref):
    parts = []
    for t in range(3):
        for r in range(3):
            k = (t * 3 + r) * 3
            parts += [w_ref[k, 0:128], w_ref[k + 1, 0:128], w_ref[k + 2, 0:128]]
            parts += [w_ref[k, 128:192], w_ref[k + 1, 128:192]]
    for t in range(3):
        parts += [w_ref[(t * 3 + r) * 3 + 2, 128:192] for r in range(3)]
        parts.append(jnp.zeros((64, w_ref.shape[-1]), BF16))
    return jnp.concatenate(parts, axis=0)


def conv_rows(s_ref, t_ref, weights, f, nf, row0, t_row0, rows):
    col = s_ref.shape[2]
    m = nf * rows * col
    parts = []
    for t in range(3):
        for r in range(3):
            parts.append(
                s_ref[pl.ds(f + t, nf), row0 + r : row0 + r + rows].reshape(m, 512)
            )
    for t in range(3):
        parts.append(t_ref[pl.ds(f + t, nf), t_row0 : t_row0 + rows].reshape(m, 256))
    return jnp.dot(jnp.concatenate(parts, axis=1), weights, preferred_element_type=F32)


def pack_kernel(x_ref, even_ref, odd_ref, stat_ref):
    odd = lax.rem(lax.axis_index("tile"), 2)
    frames, rows, cols, chan = x_ref.shape
    even_ref[...] = x_ref[:, pl.ds(1 - odd, 3)]
    odd_ref[...] = x_ref[:, pl.ds(odd, 3)]
    local_stats(
        lambda f: x_ref[f].reshape(rows * cols, chan).astype(F32),
        frames,
        rows * cols * (chan // G),
        chan,
        stat_ref,
    )


def conv_one_kernel(
    ring,
    row_list,
    x_ref,
    p1_ref,
    p2_ref,
    xc_ref,
    p1c_ref,
    p2c_ref,
    g_ref,
    gain_ref,
    shift_ref,
    w_ref,
    bias_ref,
    *rest,
):
    if ring:
        out_ref, cache_ref, stat_ref, mean_ref, scale_ref, s_ref, t_ref = rest
    else:
        out_ref, cache_ref, mean_ref, scale_ref, s_ref, t_ref = rest
    frames, rows, cols, chan = x_ref.shape
    tm, tile = lax.axis_index("tm"), lax.axis_index("tile")
    last = lax.axis_size("tile") - 1
    odd = lax.rem(tile, 2) == 1
    count = rows * cols * (chan // G)
    global_stats(g_ref, mean_ref, scale_ref, gain_ref, count)
    shift = shift_ref[...]
    t_ref[...] = jnp.zeros_like(t_ref)

    def fetch(refs, frame, row):
        own, p1, p2 = refs
        if row < 3:
            return jnp.where(odd, p1[frame, row].astype(F32), p2[frame, row].astype(F32))
        if row < 3 + rows:
            return own[frame, row - 3].astype(F32)
        row = row - 3 - rows
        return jnp.where(odd, p2[frame, row].astype(F32), p1[frame, row].astype(F32))

    def norm_frame(refs, frame, slot, index):
        mean, scale = mean_ref[index], scale_ref[index]
        place = 0
        for first, n, _ in row_list:
            for row in range(first, first + n + 2):
                v = silu((fetch(refs, frame, row) - mean) * scale + shift)
                if row < 3:
                    v = jnp.where(tile > 0, v, 0.0)
                if row >= 3 + rows:
                    v = jnp.where(tile < last, v, 0.0)
                put_run(v, slot, place, row - first, n)
            place += n + 2

    def put_run(v, slot, place, r, n):
        a, b = v[:, :128], v[:, 128:192]
        a_left, a_right = shifted(a)
        b_left, b_right = shifted(b)
        k = place + r
        s_ref[slot, k, :, 0:128] = a_left.astype(BF16)
        s_ref[slot, k, :, 128:256] = a.astype(BF16)
        s_ref[slot, k, :, 256:384] = a_right.astype(BF16)
        s_ref[slot, k, :, 384:512] = jnp.concatenate([b_left, b], axis=1).astype(BF16)
        tail = b_right.astype(BF16)
        for j in range(3):
            if 0 <= r - j < n:
                t_ref[slot, place + r - j, :, 64 * j : 64 * j + 64] = tail

    @pl.when(tm == 0)
    def _():
        s_ref[0:2] = jnp.zeros_like(s_ref[0:2])

    @pl.when(tm > 0)
    def _():
        def step(f, c):
            norm_frame((xc_ref, p1c_ref, p2c_ref), f + frames - 2, f, f + frames - 2)
            return c

        lax.fori_loop(0, 2, step, 0)

    def step(f, c):
        norm_frame((x_ref, p1_ref, p2_ref), f, f + 2, tm * frames + f)
        return c

    lax.fori_loop(0, frames, step, 0)
    weights = tap_weights(w_ref)
    bias = bias_ref[...]
    place = 0
    for first, n, where_to in row_list:
        for f in range(0, frames, 2):
            out = conv_rows(s_ref, t_ref, weights, f, 2, place, place, n) + bias
            out = out.astype(BF16).reshape(2, n, cols, chan)
            out_ref[f : f + 2, where_to : where_to + n] = out
            if f >= frames - 2:
                cache_ref[:, where_to : where_to + n] = out
        place += n + 2
    if ring:
        local_stats(
            lambda f: out_ref[f].reshape(rows * cols, chan).astype(F32),
            frames,
            count,
            chan,
            stat_ref,
        )


def conv_two_kernel(
    x_ref,
    p1_ref,
    p2_ref,
    h_ref,
    hh_ref,
    hc_ref,
    hhc_ref,
    g_ref,
    gain_ref,
    shift_ref,
    w_ref,
    bias_ref,
    wu_ref,
    bu_ref,
    out_ref,
    mean_ref,
    scale_ref,
    s_ref,
    t_ref,
    sj_ref,
    tj_ref,
):
    frames, rows, cols, chan = x_ref.shape
    tm, tile = lax.axis_index("tm"), lax.axis_index("tile")
    last = lax.axis_size("tile") - 1
    odd = lax.rem(tile, 2) == 1
    global_stats(g_ref, mean_ref, scale_ref, gain_ref, rows * cols * (chan // G))
    shift = shift_ref[...]
    t_ref[...] = jnp.zeros_like(t_ref)

    def norm_frame(own, halo, frame, slot, index):
        mean, scale = mean_ref[index], scale_ref[index]
        for row in range(rows + 4):
            if row < 2:
                v = halo[frame, row]
            elif row < rows + 2:
                v = own[frame, row - 2]
            else:
                v = halo[frame, row - rows]
            v = silu((v.astype(F32) - mean) * scale + shift)
            if row < 2:
                v = jnp.where(tile > 0, v, 0.0)
            if row >= rows + 2:
                v = jnp.where(tile < last, v, 0.0)
            put_row(v, s_ref, t_ref, slot, row, rows + 2, 3)

    @pl.when(tm == 0)
    def _():
        s_ref[0:2] = jnp.zeros_like(s_ref[0:2])

    @pl.when(tm > 0)
    def _():
        def step(f, c):
            norm_frame(hc_ref, hhc_ref, f, f, f + frames - 2)
            return c

        lax.fori_loop(0, 2, step, 0)

    def step(f, c):
        norm_frame(h_ref, hh_ref, f, f + 2, tm * frames + f)
        return c

    lax.fori_loop(0, frames, step, 0)
    weights = tap_weights(w_ref)
    bias, bias_up = bias_ref[...], bu_ref[...]

    def frame_out(f, c):
        out = conv_rows(s_ref, t_ref, weights, f, 1, 0, 0, rows + 2) + bias
        for r in range(rows + 2):
            if r == 0:
                x = jnp.where(odd, p1_ref[f, 2].astype(F32), p2_ref[f, 2].astype(F32))
            elif r <= rows:
                x = x_ref[f, r - 1].astype(F32)
            else:
                x = jnp.where(odd, p2_ref[f, 0].astype(F32), p1_ref[f, 0].astype(F32))
            v = (out[r * cols : (r + 1) * cols] + x).astype(BF16).astype(F32)
            if r == 0:
                v = jnp.where(tile > 0, v, 0.0)
            if r > rows:
                v = jnp.where(tile < last, v, 0.0)
            put_row(v, sj_ref, tj_ref, 0, r, rows + 1, 2)
        m = rows * cols
        for s in range(2):
            parts = [sj_ref[0, s + i : s + i + rows].reshape(m, 512) for i in range(2)]
            parts.append(tj_ref[0, s : s + rows].reshape(m, 128))
            up = jnp.dot(jnp.concatenate(parts, axis=1), wu_ref[s], preferred_element_type=F32)
            up = (up + bias_up).astype(BF16).reshape(rows, cols, chan)
            for y in range(rows):
                out_ref[f, 2 * y + s] = up[y]
        return c

    lax.fori_loop(0, frames, frame_out, 0)


def folded_up(up_kernel):
    k = up_kernel.astype(F32)
    zero = jnp.zeros_like(k[0, 0])
    out = []
    for rows in ((k[0], k[1] + k[2]), (k[0] + k[1], k[2])):
        taps = []
        for c in rows:
            taps.append(
                [
                    jnp.concatenate([c[0], zero], axis=1),
                    jnp.concatenate([c[1] + c[2], c[0] + c[1]], axis=1),
                    jnp.concatenate([zero, c[2]], axis=1),
                ]
            )
        parts = []
        for t in taps:
            parts += [t[0][:128], t[1][:128], t[2][:128], t[0][128:], t[1][128:]]
        parts += [t[2][128:] for t in taps]
        out.append(jnp.concatenate(parts, axis=0))
    return jnp.stack(out).astype(BF16)


def exchange(stat):
    return lax.all_to_all(stat, ("tm", "tile"), 0, 0)


def body(
    features,
    gain_one,
    shift_one,
    kernel_one,
    bias_one,
    gain_two,
    shift_two,
    kernel_two,
    bias_two,
    up_kernel,
    up_bias,
):
    x = features[0]
    frames, rows, cols, chan = x.shape
    tiles = lax.axis_size("tile")
    even_pairs = [(i, i ^ 1) for i in range(tiles)]
    odd_pairs = [(i, i + 1) for i in range(1, tiles - 1, 2)]
    odd_pairs += [(b, a) for a, b in odd_pairs]
    down = [(0, 1)]
    shape = jax.ShapeDtypeStruct
    stat_shape = shape((2 * tiles, 2, 128), F32)
    limit = pltpu.CompilerParams(vmem_limit_bytes=48 * 2**20)

    xc = lax.ppermute(x, "tm", down)
    even, odd, stat = pl.pallas_call(
        pack_kernel,
        out_shape=(
            shape((frames, 3, cols, chan), BF16),
            shape((frames, 3, cols, chan), BF16),
            stat_shape,
        ),
        in_specs=[VM],
        out_specs=(VM, VM, VM),
        compiler_params=limit,
        name="pack",
    )(x)
    p1 = lax.ppermute(even, "tile", even_pairs)
    p2 = lax.ppermute(odd, "tile", odd_pairs)
    p1c = lax.ppermute(p1, "tm", down)
    p2c = lax.ppermute(p2, "tm", down)
    all_one = exchange(stat)
    w_one = kernel_one.reshape(27, chan, chan)
    w_two = kernel_two.reshape(27, chan, chan)
    w_up = folded_up(up_kernel)
    vec = lambda v: v.reshape(1, chan)
    args = (x, p1, p2, xc, p1c, p2c, all_one, vec(gain_one), vec(shift_one), w_one, vec(bias_one))

    def conv_one(ring, row_list):
        in_rows = sum(n + 2 for _, n, _ in row_list)
        outs = (shape((frames, rows, cols, chan), BF16), shape((2, rows, cols, chan), BF16))
        if ring:
            outs += (stat_shape,)
        flops = 2 * frames * rows * cols * 27 * chan * chan
        return pl.pallas_call(
            functools.partial(conv_one_kernel, ring, row_list),
            out_shape=outs,
            in_specs=[VM] * len(args),
            out_specs=(VM,) * len(outs),
            scratch_shapes=[
                pltpu.VMEM((8, 1, chan), F32),
                pltpu.VMEM((8, 1, chan), F32),
                pltpu.VMEM((frames + 2, in_rows, cols, 512), BF16),
                pltpu.VMEM((frames + 2, in_rows, cols, 256), BF16),
            ],
            compiler_params=limit,
            cost_estimate=pl.CostEstimate(
                flops=flops, bytes_accessed=4 * 2**20, transcendentals=0
            ),
            name="conv_one" if ring else "conv_one_rim",
        )(*args)

    hidden, hidden_c, stat_two = conv_one(True, ((2, rows, 0),))
    all_two = exchange(stat_two)
    rim, rim_c = conv_one(False, ((0, 2, 0), (rows + 2, 2, 2)))
    hc = lax.ppermute(hidden_c, "tm", down)
    rim_cc = lax.ppermute(rim_c, "tm", down)
    bias_up = jnp.concatenate([up_bias, up_bias]).reshape(1, chan)
    out = pl.pallas_call(
        conv_two_kernel,
        out_shape=shape((frames, 2 * rows, cols, chan), BF16),
        in_specs=[VM] * 14,
        out_specs=VM,
        scratch_shapes=[
            pltpu.VMEM((8, 1, chan), F32),
            pltpu.VMEM((8, 1, chan), F32),
            pltpu.VMEM((frames + 2, rows + 4, cols, 512), BF16),
            pltpu.VMEM((frames + 2, rows + 2, cols, 256), BF16),
            pltpu.VMEM((1, rows + 2, cols, 512), BF16),
            pltpu.VMEM((1, rows + 1, cols, 128), BF16),
        ],
        compiler_params=limit,
        cost_estimate=pl.CostEstimate(
            flops=3 * frames * rows * cols * 27 * chan * chan,
            bytes_accessed=4 * 2**20,
            transcendentals=0,
        ),
        name="conv_two",
    )(
        x, p1, p2, hidden, rim, hc, rim_cc, all_two,
        vec(gain_two), vec(shift_two), w_two, vec(bias_two), w_up, bias_up,
    )
    return out[None]


def solution(mesh):
    return jax.shard_map(
        body,
        mesh=mesh,
        in_specs=(P(None, "tm", "tile", None, None),) + (P(),) * 10,
        out_specs=P(None, "tm", "tile", None, None),
        check_vma=False,
    )
```

```python
import functools

import jax
import jax.numpy as jnp
from jax import lax
from jax.experimental import pallas as pl
from jax.experimental.pallas import tpu as pltpu
from jax.sharding import PartitionSpec as P

G = 32
EPS = 1e-06
LIMIT = 52 * 2**20
FOLD_FLOPS = 10**10
RIM_FLOPS = 10**10
TABLE_FLOPS = 2 * 10**10
F32 = jnp.float32
BF16 = jnp.bfloat16
VM = pl.BlockSpec(memory_space=pltpu.VMEM)
HB = pl.BlockSpec(memory_space=pltpu.HBM)


def dot01(a, b):
    high = a.astype(BF16).astype(F32)
    rest = a - high
    middle = rest.astype(BF16).astype(F32)
    parts = jnp.concatenate([high, middle, rest - middle], axis=0).astype(BF16)
    out = jnp.dot(parts, b, preferred_element_type=F32)
    return out[0:8] + out[8:16] + out[16:24]


def spread(chan):
    lane = lax.broadcasted_iota(jnp.int32, (128, chan), 0)
    col = lax.broadcasted_iota(jnp.int32, (128, chan), 1)
    low = (lane & (G - 1)) * (chan // G)
    return jnp.where((col >= low) & (col < low + chan // G), 1.0, 0.0).astype(BF16)


def gather_groups(chan):
    lane = lax.broadcasted_iota(jnp.int32, (chan, 128), 1)
    col = lax.broadcasted_iota(jnp.int32, (chan, 128), 0)
    low = (lane & (G - 1)) * (chan // G)
    return jnp.where((col >= low) & (col < low + chan // G), 1.0, 0.0).astype(BF16)


def frame_mask(first):
    lane = lax.broadcasted_iota(jnp.int32, (8, 128), 1)
    row = lax.broadcasted_iota(jnp.int32, (8, 128), 0)
    low = (row - first) * G
    return (lane >= low) & (lane < low + G)


def stack_rows(rows):
    width = rows[0].shape[1]
    index = lax.broadcasted_iota(jnp.int32, (8, width), 0)
    out = jnp.zeros((8, width), F32)
    for i, r in enumerate(rows):
        out = jnp.where(index == i, jnp.broadcast_to(r, (8, width)), out)
    return out


def channel_stats(v):
    mean = jnp.sum(v, axis=0, keepdims=True) / v.shape[0]
    off = v - mean
    return mean, jnp.sum(off * off, axis=0, keepdims=True)


def local_stats(stats, positions, stat_ref):
    chan = stats[0][0].shape[1]
    mask = frame_mask(0)
    to_group, to_chan = gather_groups(chan), spread(chan)
    means = stack_rows([m for m, _ in stats])
    squares = stack_rows([q for _, q in stats])
    mean = jnp.where(mask, dot01(means, to_group), 0.0) / (chan // G)
    off = means - dot01(mean, to_chan)
    square = jnp.where(mask, dot01(squares + positions * off * off, to_group), 0.0)
    packed = jnp.concatenate(
        [jnp.sum(mean, axis=0, keepdims=True), jnp.sum(square, axis=0, keepdims=True)], axis=0
    )
    stat_ref[...] = jnp.broadcast_to(packed[None], stat_ref.shape)


def table_kernel(count, stat_ref, gain_ref, mean_ref, scale_ref):
    gain = gain_ref[...]
    tiles = stat_ref.shape[0] // 2
    chan = mean_ref.shape[-1]
    to_chan = spread(chan)
    means, spreads = [], []
    for half in range(2):
        part = stat_ref[half * tiles : (half + 1) * tiles]
        total = jnp.sum(part, axis=0)
        mean = total[0:1] / tiles
        off = part - mean[None]
        spread_sum = total[1:2] + count * jnp.sum(off * off, axis=0)[0:1]
        means.append(mean)
        spreads.append(spread_sum / (tiles * count))
    m0, m1 = frame_mask(0), frame_mask(4)
    mean8 = jnp.where(m0, means[0], 0.0) + jnp.where(m1, means[1], 0.0)
    inv8 = jnp.where(m0, lax.rsqrt(spreads[0] + EPS), 0.0) + jnp.where(
        m1, lax.rsqrt(spreads[1] + EPS), 0.0
    )
    mean_chan = dot01(mean8, to_chan)
    scale = dot01(inv8, to_chan) * gain
    for f in range(8):
        mean_ref[f] = mean_chan[f : f + 1]
        scale_ref[f] = scale[f : f + 1]


def columns(shape, cols):
    return lax.broadcasted_iota(jnp.int32, shape, 0) & (cols - 1)


def from_left(v, cols):
    return jnp.where(columns(v.shape, cols) == 0, 0.0, pltpu.roll(v, 1, axis=0))


def from_right(v, cols):
    turned = pltpu.roll(v, v.shape[0] - 1, axis=0)
    return jnp.where(columns(v.shape, cols) == cols - 1, 0.0, turned)


def put_row(v, a_ref, b_ref, f, k):
    tail = v[:, 128:192].astype(BF16)
    a_ref[f, k] = v[:, 0:128].astype(BF16)
    b_ref[f, k, :, 0:64] = tail
    if k > 0:
        b_ref[f, k - 1, :, 64:128] = tail
    return tail


def silu(u):
    half = 0.5 * u
    return half + half * jnp.tanh(half)


def conv_rows(a_ref, b_ref, d_ref, w_ref, f, runs, cols):
    def take(ref, slot, r):
        parts = [ref[slot, k + r : k + r + n].reshape(n * cols, 128) for k, n in runs]
        return parts[0] if len(parts) == 1 else jnp.concatenate(parts, axis=0)

    parts = [take(a_ref, f + t, r) for t in range(3) for r in range(3)]
    parts += [take(b_ref, f + t, 0) for t in range(3)]
    parts += [take(d_ref, f, 2), take(b_ref, f + 2, 2)]
    maps = jnp.concatenate(parts, axis=1)

    def taps(k):
        low, high = slice(0, 128), slice(128, 192)
        at = lambda t, r: (t * 3 + r) * 3 + k
        rows = [w_ref[at(t, r), low] for t in range(3) for r in range(3)]
        for t in range(3):
            rows += [w_ref[at(t, 0), high], w_ref[at(t, 1), high]]
        rows += [w_ref[at(0, 2), high], w_ref[at(1, 2), high], w_ref[at(2, 2), high]]
        rows.append(jnp.zeros((64, w_ref.shape[-1]), BF16))
        return jnp.concatenate(rows, axis=0)

    left, centre, right = [
        jnp.dot(maps, taps(k), preferred_element_type=F32) for k in range(3)
    ]
    return centre + from_left(left, cols) + from_right(right, cols)


class Copies:
    def __init__(self, pairs, sems):
        self.pending = {}
        for i, (key, source, target) in enumerate(pairs):
            copy = pltpu.make_async_copy(source, target, sems.at[i])
            copy.start()
            self.pending[key] = copy

    def need(self, *keys):
        for key in keys:
            if key in self.pending:
                self.pending.pop(key).wait()


def pack_kernel(x_ref, even_ref, odd_ref, stat_ref):
    odd = lax.rem(lax.axis_index("tile"), 2)
    frames, rows, cols, chan = x_ref.shape
    even_ref[...] = x_ref[:, pl.ds(1 - odd, 3)]
    odd_ref[...] = x_ref[:, pl.ds(odd, 3)]
    stats = [
        channel_stats(x_ref[f].reshape(rows * cols, chan).astype(F32)) for f in range(frames)
    ]
    local_stats(stats, rows * cols, stat_ref)


def fold_kernel(x_ref, p1_ref, p2_ref, k_ref, wu_ref, c_ref):
    frames, rows = x_ref.shape[:2]
    c_ref[:, 0:3] = p1_ref[frames - 2 :]
    c_ref[:, 3 : 3 + rows] = x_ref[frames - 2 :]
    c_ref[:, 3 + rows :] = p2_ref[frames - 2 :]
    k = [[k_ref[3 * j + i].astype(F32) for i in range(3)] for j in range(3)]
    plus = lambda p, q: [a + b for a, b in zip(p, q)]
    for s, taps in enumerate(((k[0], plus(k[1], k[2])), (plus(k[0], k[1]), k[2]))):
        for i, c in enumerate(taps):
            sides = jnp.concatenate([c[0], c[2]], axis=1).astype(BF16)
            centre = jnp.concatenate([c[1] + c[2], c[0] + c[1]], axis=1).astype(BF16)
            for j, v in enumerate((sides, centre)):
                wu_ref[s, j, 128 * i : 128 * i + 128] = v[:128]
                wu_ref[s, j, 256 + 64 * i : 320 + 64 * i] = v[128:]


def conv_one_kernel(ring, row_list, x_hbm, p1_hbm, p2_hbm, c_hbm, w_hbm, vec_ref, mean_ref, scale_ref, *rest):
    if ring:
        out_ref, stat_ref = rest[:2]
    else:
        h_hbm, out_ref, cache_ref = rest[:3]
    x_ref, p1_ref, p2_ref, c_ref, w_ref, a_ref, b_ref, d_ref, sems = rest[-9:]
    frames, rows, cols, chan = x_ref.shape
    pairs = [
        ("c", c_hbm, c_ref),
        ("x", x_hbm, x_ref),
        ("p1", p1_hbm, p1_ref),
        ("p2", p2_hbm, p2_ref),
        ("w", w_hbm, w_ref),
    ]
    if not ring:
        pairs.append(("h", h_hbm.at[pl.ds(frames - 2, 2)], cache_ref.at[:, pl.ds(2, rows)]))
    copies = Copies(pairs, sems)
    tm, tile = lax.axis_index("tm"), lax.axis_index("tile")
    last = lax.axis_size("tile") - 1
    odd = lax.rem(tile, 2) == 1
    shift, bias = vec_ref[0:1], vec_ref[1:2]
    in_rows = a_ref.shape[1]
    b_ref[:, in_rows - 1] = jnp.zeros_like(b_ref[:, in_rows - 1])

    def fetch(slot, row):
        if slot < 2:
            if 3 <= row < 3 + rows:
                return c_ref[slot, row].astype(F32)
            other = row + 3 + rows if row < 3 else row - 3 - rows
            return jnp.where(odd, c_ref[slot, row].astype(F32), c_ref[slot, other].astype(F32))
        frame = slot - 2
        if 3 <= row < 3 + rows:
            return x_ref[frame, row - 3].astype(F32)
        k = row if row < 3 else row - 3 - rows
        p1, p2 = p1_ref[frame, k].astype(F32), p2_ref[frame, k].astype(F32)
        return jnp.where(odd == (row < 3), p1, p2)

    def norm_frame(slot):
        index = slot + frames - 2 if slot < 2 else tm * frames + slot - 2
        mean, scale = mean_ref[index], scale_ref[index]
        k = 0
        for first, n, _ in row_list:
            for row in range(first, first + n + 2):
                v = silu((fetch(slot, row) - mean) * scale + shift)
                keep = None
                if row < 3:
                    keep = tile > 0
                if row >= 3 + rows:
                    keep = tile < last
                if slot < 2:
                    keep = (tm > 0) if keep is None else keep & (tm > 0)
                if keep is not None:
                    v = jnp.where(keep, v, 0.0)
                put_both(put_row(v, a_ref, b_ref, slot, k), d_ref, slot, k)
                k += 1

    copies.need("c")
    norm_frame(0)
    norm_frame(1)
    copies.need("x", "p1", "p2")
    stats, runs, k = [], [], 0
    for _, n, _ in row_list:
        runs.append((k, n))
        k += n + 2
    for f in range(frames):
        norm_frame(f + 2)
        copies.need("w")
        out = (conv_rows(a_ref, b_ref, d_ref, w_ref, f, runs, cols) + bias).astype(BF16)
        rows_out = out.reshape(rows, cols, chan)
        k = 0
        for _, n, where_to in row_list:
            out_ref[f, where_to : where_to + n] = rows_out[k : k + n]
            if not ring and f >= frames - 2:
                at = where_to if where_to == 0 else where_to + rows
                cache_ref[f - frames + 2, at : at + n] = rows_out[k : k + n]
            k += n
        if ring:
            stats.append(channel_stats(out.astype(F32)))
    if ring:
        local_stats(stats, rows * cols, stat_ref)
    copies.need("h")


def put_both(tail, d_ref, slot, k):
    if slot < d_ref.shape[0]:
        d_ref[slot, k, :, 0:64] = tail
    if 0 < slot <= d_ref.shape[0]:
        d_ref[slot - 1, k, :, 64:128] = tail


def conv_two_kernel(
    x_hbm,
    p1_hbm,
    p2_hbm,
    h_hbm,
    hh_hbm,
    hc_hbm,
    w_hbm,
    wu_hbm,
    vec_ref,
    mean_ref,
    scale_ref,
    out_hbm,
    x_ref,
    p1_ref,
    p2_ref,
    h_ref,
    hh_ref,
    hc_ref,
    w_ref,
    wu_ref,
    out_ref,
    a_ref,
    b_ref,
    d_ref,
    aj_ref,
    bj_ref,
    sems,
    out_sems,
):
    frames, rows, cols, chan = x_ref.shape
    copies = Copies(
        [
                ("hc", hc_hbm, hc_ref),
            ("h", h_hbm, h_ref),
            ("hh", hh_hbm, hh_ref),
            ("w", w_hbm, w_ref),
            ("x", x_hbm, x_ref),
            ("p1", p1_hbm, p1_ref),
            ("p2", p2_hbm, p2_ref),
            ("wu", wu_hbm, wu_ref),
        ],
        sems,
    )
    tm, tile = lax.axis_index("tm"), lax.axis_index("tile")
    last = lax.axis_size("tile") - 1
    odd = lax.rem(tile, 2) == 1
    shift, bias, bias_up = vec_ref[2:3], vec_ref[3:4], vec_ref[4:5]
    in_rows = a_ref.shape[1]
    b_ref[:, in_rows - 1] = jnp.zeros_like(b_ref[:, in_rows - 1])

    def norm_frame(slot):
        index = slot + frames - 2 if slot < 2 else tm * frames + slot - 2
        mean, scale = mean_ref[index], scale_ref[index]
        for row in range(rows + 4):
            if slot < 2:
                v = hc_ref[slot, row]
            elif row < 2:
                v = hh_ref[slot - 2, row]
            elif row < rows + 2:
                v = h_ref[slot - 2, row - 2]
            else:
                v = hh_ref[slot - 2, row - rows]
            v = silu((v.astype(F32) - mean) * scale + shift)
            keep = None
            if row < 2:
                keep = tile > 0
            if row >= rows + 2:
                keep = tile < last
            if slot < 2:
                keep = (tm > 0) if keep is None else keep & (tm > 0)
            if keep is not None:
                v = jnp.where(keep, v, 0.0)
            put_both(put_row(v, a_ref, b_ref, slot, row), d_ref, slot, row)

    def joined_frame(f):
        copies.need("w")
        out = conv_rows(a_ref, b_ref, d_ref, w_ref, f, [(0, rows + 2)], cols) + bias
        copies.need("x", "p1", "p2")
        for r in range(rows + 2):
            if r == 0:
                x = jnp.where(odd, p1_ref[f, 2].astype(F32), p2_ref[f, 2].astype(F32))
            elif r <= rows:
                x = x_ref[f, r - 1].astype(F32)
            else:
                x = jnp.where(odd, p2_ref[f, 0].astype(F32), p1_ref[f, 0].astype(F32))
            v = out[r * cols : (r + 1) * cols] + x
            if r == 0:
                v = jnp.where(tile > 0, v, 0.0)
            if r > rows:
                v = jnp.where(tile < last, v, 0.0)
            put_row(v, aj_ref, bj_ref, f, r)

    def up_frame(f):
        copies.need("wu")
        m = rows * cols
        first = lax.broadcasted_iota(jnp.int32, (m, chan), 1) < chan // 2
        for s in range(2):
            parts = [aj_ref[f, s + i : s + i + rows].reshape(m, 128) for i in range(2)]
            parts.append(bj_ref[f, s : s + rows].reshape(m, 128))
            maps = jnp.concatenate(parts, axis=1)
            sides = jnp.dot(maps, wu_ref[s, 0], preferred_element_type=F32)
            up = jnp.dot(maps, wu_ref[s, 1], preferred_element_type=F32)
            up = up + jnp.where(first, from_left(sides, cols), from_right(sides, cols))
            up = (up + bias_up).astype(BF16).reshape(rows, cols, chan)
            for y in range(rows):
                out_ref[f, 2 * y + s] = up[y]

    copies.need("hc")
    norm_frame(0)
    norm_frame(1)
    copies.need("h", "hh")
    norm_frame(2)
    written = []
    for f in range(frames):
        joined_frame(f)
        if f + 3 < frames + 2:
            norm_frame(f + 3)
        up_frame(f)
        copy = pltpu.make_async_copy(out_ref.at[f], out_hbm.at[f], out_sems.at[f])
        copy.start()
        written.append(copy)
    for copy in written:
        copy.wait()


def exchange(stat):
    return lax.all_to_all(stat, ("tm", "tile"), 0, 0)


def body(
    features,
    gain_one,
    shift_one,
    kernel_one,
    bias_one,
    gain_two,
    shift_two,
    kernel_two,
    bias_two,
    up_kernel,
    up_bias,
):
    x = features[0]
    frames, rows, cols, chan = x.shape
    tiles = lax.axis_size("tile")
    even_pairs = [(i, i ^ 1) for i in range(tiles)]
    odd_pairs = [(i, i + 1) for i in range(1, tiles - 1, 2)]
    odd_pairs += [(b, a) for a, b in odd_pairs]
    down = [(0, 1)]
    shape = jax.ShapeDtypeStruct
    stat_shape = shape((2 * tiles, 2, 128), F32)
    small = pltpu.CompilerParams(vmem_limit_bytes=12 * 2**20)
    limit = pltpu.CompilerParams(vmem_limit_bytes=LIMIT)
    one_conv = 2 * frames * rows * cols * 27 * chan * chan
    cost = lambda flops, moved: pl.CostEstimate(
        flops=flops, bytes_accessed=moved, transcendentals=0
    )

    even, odd, stat = pl.pallas_call(
        pack_kernel,
        out_shape=(
            shape((frames, 3, cols, chan), BF16),
            shape((frames, 3, cols, chan), BF16),
            stat_shape,
        ),
        in_specs=[VM],
        out_specs=(VM, VM, VM),
        compiler_params=small,
        name="pack",
    )(x)
    p1 = lax.ppermute(even, "tile", even_pairs)
    p2 = lax.ppermute(odd, "tile", odd_pairs)
    all_one = exchange(stat)
    w_one = kernel_one.reshape(27, chan, chan)
    w_two = kernel_two.reshape(27, chan, chan)
    w_up, last_two = pl.pallas_call(
        fold_kernel,
        out_shape=(
            shape((2, 2, 2 * chan, chan), BF16),
            shape((2, rows + 6, cols, chan), BF16),
        ),
        in_specs=[VM] * 4,
        out_specs=(VM, VM),
        compiler_params=small,
        cost_estimate=cost(FOLD_FLOPS, 4 * 2**20),
        name="fold",
    )(x, p1, p2, up_kernel.reshape(9, chan, chan // 2))
    before = lax.ppermute(last_two, "tm", down)
    vectors = jnp.stack(
        [shift_one, bias_one, shift_two, bias_two, jnp.concatenate([up_bias, up_bias])]
    )

    def table(stats, gain):
        rows_of = shape((8, 1, chan), F32)
        return pl.pallas_call(
            functools.partial(table_kernel, rows * cols * (chan // G)),
            out_shape=(rows_of, rows_of),
            in_specs=[VM, VM],
            out_specs=(VM, VM),
            compiler_params=small,
            cost_estimate=cost(TABLE_FLOPS, 2**18),
            name="table",
        )(stats, gain.reshape(1, chan))

    def scratch(in_rows, out_frames):
        return [
            pltpu.VMEM((frames + 2, in_rows, cols, 128), BF16),
            pltpu.VMEM((frames + 2, in_rows, cols, 128), BF16),
            pltpu.VMEM((frames, in_rows, cols, 128), BF16),
        ]

    held = lambda v: pltpu.VMEM(v.shape, v.dtype)
    args = (x, p1, p2, before, w_one)
    table_one = table(all_one, gain_one)

    def conv_one(ring, row_list, *more):
        outs = (shape((frames, rows, cols, chan), BF16),)
        outs += (stat_shape,) if ring else (shape((2, rows + 4, cols, chan), BF16),)
        return pl.pallas_call(
            functools.partial(conv_one_kernel, ring, row_list),
            out_shape=outs,
            in_specs=[HB] * len(args) + [VM] * 3 + [HB] * len(more),
            out_specs=(VM,) * len(outs),
            scratch_shapes=[held(v) for v in args]
            + scratch(sum(n + 2 for _, n, _ in row_list), frames)
            + [pltpu.SemaphoreType.DMA((7,))],
            compiler_params=limit,
            cost_estimate=cost(one_conv if ring else RIM_FLOPS, 4 * 2**20),
            name="conv_one" if ring else "conv_one_rim",
        )(*args, vectors, *table_one, *more)

    hidden, stat_two = conv_one(True, ((2, rows, 0),))
    all_two = exchange(stat_two)
    rim, hidden_two = conv_one(False, ((0, 2, 0), (rows + 2, 2, 2)), hidden)
    hidden_before = lax.ppermute(hidden_two, "tm", down)
    args_two = (x, p1, p2, hidden, rim, hidden_before, w_two, w_up)
    out_shape = shape((frames, 2 * rows, cols, chan), BF16)
    out = pl.pallas_call(
        conv_two_kernel,
        out_shape=out_shape,
        in_specs=[HB] * len(args_two) + [VM] * 3,
        out_specs=HB,
        scratch_shapes=[held(v) for v in args_two]
        + [held(out_shape)]
        + scratch(rows + 4, frames)
        + [
            pltpu.VMEM((frames, rows + 2, cols, 128), BF16),
            pltpu.VMEM((frames, rows + 2, cols, 128), BF16),
            pltpu.SemaphoreType.DMA((9,)),
            pltpu.SemaphoreType.DMA((frames,)),
        ],
        compiler_params=limit,
        cost_estimate=cost(3 * one_conv, 4 * 2**20),
        name="conv_two",
    )(*args_two, vectors, *table(all_two, gain_two))
    return out[None]


def solution(mesh):
    return jax.shard_map(
        body,
        mesh=mesh,
        in_specs=(P(None, "tm", "tile", None, None),) + (P(),) * 10,
        out_specs=P(None, "tm", "tile", None, None),
        check_vma=False,
    )
```

```python
import functools

import jax
import jax.numpy as jnp
from jax import lax
from jax.experimental import pallas as pl
from jax.experimental.pallas import tpu as pltpu
from jax.sharding import PartitionSpec as P

G = 32
EPS = 1e-06
LIMIT = 24 * 2**20
FILL_FLOPS = 15 * 10**9
RIM_FLOPS = 4 * 10**9
TABLE_FLOPS = 1500000000
F32 = jnp.float32
BF16 = jnp.bfloat16
VM = pl.BlockSpec(memory_space=pltpu.VMEM)
HB = pl.BlockSpec(memory_space=pltpu.HBM)


def dot01(a, b):
    high = a.astype(BF16).astype(F32)
    rest = a - high
    middle = rest.astype(BF16).astype(F32)
    parts = jnp.concatenate([high, middle, rest - middle], axis=0).astype(BF16)
    out = jnp.dot(parts, b, preferred_element_type=F32)
    return out[0:8] + out[8:16] + out[16:24]


def spread(chan):
    lane = lax.broadcasted_iota(jnp.int32, (128, chan), 0)
    col = lax.broadcasted_iota(jnp.int32, (128, chan), 1)
    low = (lane & (G - 1)) * (chan // G)
    return jnp.where((col >= low) & (col < low + chan // G), 1.0, 0.0).astype(BF16)


def gather_groups(chan):
    lane = lax.broadcasted_iota(jnp.int32, (chan, 128), 1)
    col = lax.broadcasted_iota(jnp.int32, (chan, 128), 0)
    low = (lane & (G - 1)) * (chan // G)
    return jnp.where((col >= low) & (col < low + chan // G), 1.0, 0.0).astype(BF16)


def frame_mask(first):
    lane = lax.broadcasted_iota(jnp.int32, (8, 128), 1)
    row = lax.broadcasted_iota(jnp.int32, (8, 128), 0)
    low = (row - first) * G
    return (lane >= low) & (lane < low + G)


def stack_rows(rows):
    width = rows[0].shape[1]
    index = lax.broadcasted_iota(jnp.int32, (8, width), 0)
    out = jnp.zeros((8, width), F32)
    for i, r in enumerate(rows):
        out = jnp.where(index == i, jnp.broadcast_to(r, (8, width)), out)
    return out


def channel_stats(v):
    mean = jnp.sum(v, axis=0, keepdims=True) / v.shape[0]
    off = v - mean
    return mean, jnp.sum(off * off, axis=0, keepdims=True)


def local_stats(stats, positions, stat_ref):
    chan = stats[0][0].shape[1]
    mask = frame_mask(0)
    to_group, to_chan = gather_groups(chan), spread(chan)
    means = stack_rows([m for m, _ in stats])
    squares = stack_rows([q for _, q in stats])
    mean = jnp.where(mask, dot01(means, to_group), 0.0) / (chan // G)
    off = means - dot01(mean, to_chan)
    square = jnp.where(mask, dot01(squares + positions * off * off, to_group), 0.0)
    packed = jnp.concatenate(
        [jnp.sum(mean, axis=0, keepdims=True), jnp.sum(square, axis=0, keepdims=True)], axis=0
    )
    stat_ref[...] = jnp.broadcast_to(packed[None], stat_ref.shape)


def table_kernel(count, stat_ref, gain_ref, mean_ref, scale_ref):
    gain = gain_ref[...]
    tiles = stat_ref.shape[0] // 2
    chan = mean_ref.shape[-1]
    to_chan = spread(chan)
    means, spreads = [], []
    for half in range(2):
        part = stat_ref[half * tiles : (half + 1) * tiles]
        total = jnp.sum(part, axis=0)
        mean = total[0:1] / tiles
        off = part - mean[None]
        spread_sum = total[1:2] + count * jnp.sum(off * off, axis=0)[0:1]
        means.append(mean)
        spreads.append(spread_sum / (tiles * count))
    m0, m1 = frame_mask(0), frame_mask(4)
    mean8 = jnp.where(m0, means[0], 0.0) + jnp.where(m1, means[1], 0.0)
    inv8 = jnp.where(m0, lax.rsqrt(spreads[0] + EPS), 0.0) + jnp.where(
        m1, lax.rsqrt(spreads[1] + EPS), 0.0
    )
    mean_chan = dot01(mean8, to_chan)
    scale = dot01(inv8, to_chan) * gain
    for f in range(8):
        mean_ref[f] = mean_chan[f : f + 1]
        scale_ref[f] = scale[f : f + 1]


def columns(shape, cols):
    return lax.broadcasted_iota(jnp.int32, shape, 0) & (cols - 1)


def from_left(v, cols):
    return jnp.where(columns(v.shape, cols) == 0, 0.0, pltpu.roll(v, 1, axis=0))


def from_right(v, cols):
    turned = pltpu.roll(v, v.shape[0] - 1, axis=0)
    return jnp.where(columns(v.shape, cols) == cols - 1, 0.0, turned)


def put_row(v, a_ref, b_ref, f, k):
    tail = v[:, 128:192].astype(BF16)
    a_ref[f, k] = v[:, 0:128].astype(BF16)
    b_ref[f, k, :, 0:64] = tail
    if k > 0:
        b_ref[f, k - 1, :, 64:128] = tail
    return tail


def silu(u):
    half = 0.5 * u
    return half + half * jnp.tanh(half)


def conv_rows(a_ref, b_ref, d_ref, w_ref, runs, cols):
    def take(ref, t, r):
        parts = [ref[f + t, k + r : k + r + n].reshape(n * cols, 128) for f, k, n in runs]
        return parts[0] if len(parts) == 1 else jnp.concatenate(parts, axis=0)

    parts = [take(a_ref, t, r) for t in range(3) for r in range(3)]
    parts += [take(b_ref, t, 0) for t in range(3)]
    parts += [take(d_ref, 0, 2), take(b_ref, 2, 2)]
    maps = jnp.concatenate(parts, axis=1)

    def taps(k):
        low, high = slice(0, 128), slice(128, 192)
        at = lambda t, r: (t * 3 + r) * 3 + k
        rows = [w_ref[at(t, r), low] for t in range(3) for r in range(3)]
        for t in range(3):
            rows += [w_ref[at(t, 0), high], w_ref[at(t, 1), high]]
        rows += [w_ref[at(0, 2), high], w_ref[at(1, 2), high], w_ref[at(2, 2), high]]
        rows.append(jnp.zeros((64, w_ref.shape[-1]), BF16))
        return jnp.concatenate(rows, axis=0)

    left, centre, right = [
        jnp.dot(maps, taps(k), preferred_element_type=F32) for k in range(3)
    ]
    return centre + from_left(left, cols) + from_right(right, cols)


def pack_kernel(x_ref, even_ref, odd_ref, stat_ref):
    odd = lax.rem(lax.axis_index("tile"), 2)
    frames, rows, cols, chan = x_ref.shape
    even_ref[...] = x_ref[:, pl.ds(1 - odd, 3)]
    odd_ref[...] = x_ref[:, pl.ds(odd, 3)]
    stats = [
        channel_stats(x_ref[f].reshape(rows * cols, chan).astype(F32)) for f in range(frames)
    ]
    local_stats(stats, rows * cols, stat_ref)


def assemble_kernel(x_ref, p1_ref, p2_ref, own_ref, c_ref):
    frames, rows = x_ref.shape[:2]
    odd = lax.rem(lax.axis_index("tile"), 2) == 1
    for f in range(frames):
        for r in range(3):
            p1, p2 = p1_ref[f, r].astype(F32), p2_ref[f, r].astype(F32)
            own_ref[f, r] = jnp.where(odd, p1, p2).astype(BF16)
            own_ref[f, 3 + rows + r] = jnp.where(odd, p2, p1).astype(BF16)
    own_ref[:, 3 : 3 + rows] = x_ref[...]
    c_ref[...] = own_ref[frames - 2 :]


def vectors_kernel(*refs):
    for i, ref in enumerate(refs[:-1]):
        refs[-1][i : i + 1, 0 : ref.shape[1]] = ref[...]
    half = refs[-2].shape[1]
    refs[-1][len(refs) - 2 : len(refs) - 1, half : 2 * half] = refs[-2][...]


def fold_kernel(k_ref, after_hbm, wu_ref):
    k = [[k_ref[3 * j + i].astype(F32) for i in range(3)] for j in range(3)]
    plus = lambda p, q: [a + b for a, b in zip(p, q)]
    for s, taps in enumerate(((k[0], plus(k[1], k[2])), (plus(k[0], k[1]), k[2]))):
        for i, c in enumerate(taps):
            sides = jnp.concatenate([c[0], c[2]], axis=1).astype(BF16)
            centre = jnp.concatenate([c[1] + c[2], c[0] + c[1]], axis=1).astype(BF16)
            for j, v in enumerate((sides, centre)):
                wu_ref[s, j, 128 * i : 128 * i + 128] = v[:128]
                wu_ref[s, j, 256 + 64 * i : 320 + 64 * i] = v[128:]


def conv_one_kernel(
    ring, row_list, own_ref, c_ref, w_ref, vec_ref, mean_ref, scale_ref, *rest
):
    if ring:
        out_ref, stat_ref, a_ref, b_ref, d_ref = rest
    else:
        h_hbm, out_ref, cache_ref, a_ref, b_ref, d_ref, sem = rest
    frames, rows, cols, chan = own_ref.shape
    rows -= 6
    if not ring:
        load_h = pltpu.make_async_copy(
            h_hbm.at[pl.ds(frames - 2, 2)], cache_ref.at[:, pl.ds(2, rows)], sem
        )
        load_h.start()
    tm, tile = lax.axis_index("tm"), lax.axis_index("tile")
    last = lax.axis_size("tile") - 1
    shift, bias = vec_ref[0:1], vec_ref[1:2]
    in_rows = a_ref.shape[1]
    b_ref[:, in_rows - 1] = jnp.zeros_like(b_ref[:, in_rows - 1])

    def fetch(slot, row):
        v = c_ref[slot, row] if slot < 2 else own_ref[slot - 2, row]
        return v.astype(F32)

    def norm_frame(slot):
        index = slot + frames - 2 if slot < 2 else tm * frames + slot - 2
        mean, scale = mean_ref[index], scale_ref[index]
        k = 0
        for first, n, _ in row_list:
            for row in range(first, first + n + 2):
                v = silu((fetch(slot, row) - mean) * scale + shift)
                keep = None
                if row < 3:
                    keep = tile > 0
                if row >= 3 + rows:
                    keep = tile < last
                if slot < 2:
                    keep = (tm > 0) if keep is None else keep & (tm > 0)
                if keep is not None:
                    v = jnp.where(keep, v, 0.0)
                put_both(put_row(v, a_ref, b_ref, slot, k), d_ref, slot, k)
                k += 1

    norm_frame(0)
    norm_frame(1)
    stats, runs, k = [], [], 0
    for _, n, _ in row_list:
        runs.append((k, n))
        k += n + 2
    for f in range(frames):
        norm_frame(f + 2)
        here = [(f, first, n) for first, n in runs]
        out = (conv_rows(a_ref, b_ref, d_ref, w_ref, here, cols) + bias).astype(BF16)
        rows_out = out.reshape(rows, cols, chan)
        k = 0
        for _, n, where_to in row_list:
            out_ref[f, where_to : where_to + n] = rows_out[k : k + n]
            if not ring and f >= frames - 2:
                at = where_to if where_to == 0 else where_to + rows
                cache_ref[f - frames + 2, at : at + n] = rows_out[k : k + n]
            k += n
        if ring:
            stats.append(channel_stats(out.astype(F32)))
    if ring:
        local_stats(stats, rows * cols, stat_ref)
    else:
        load_h.wait()


def put_both(tail, d_ref, slot, k):
    if slot < d_ref.shape[0]:
        d_ref[slot, k, :, 0:64] = tail
    if 0 < slot <= d_ref.shape[0]:
        d_ref[slot - 1, k, :, 64:128] = tail


def conv_two_kernel(
    own_ref,
    h_ref,
    hh_ref,
    hc_ref,
    w_ref,
    wu_ref,
    vec_ref,
    mean_ref,
    scale_ref,
    out_hbm,
    out_ref,
    a_ref,
    b_ref,
    d_ref,
    aj_ref,
    bj_ref,
    out_sems,
):
    frames, rows, cols, chan = h_ref.shape
    tm, tile = lax.axis_index("tm"), lax.axis_index("tile")
    last = lax.axis_size("tile") - 1
    shift, bias, bias_up = vec_ref[2:3], vec_ref[3:4], vec_ref[4:5]
    in_rows = a_ref.shape[1]
    b_ref[:, in_rows - 1] = jnp.zeros_like(b_ref[:, in_rows - 1])

    def norm_frame(slot):
        index = slot + frames - 2 if slot < 2 else tm * frames + slot - 2
        mean, scale = mean_ref[index], scale_ref[index]
        for row in range(rows + 4):
            if slot < 2:
                v = hc_ref[slot, row]
            elif row < 2:
                v = hh_ref[slot - 2, row]
            elif row < rows + 2:
                v = h_ref[slot - 2, row - 2]
            else:
                v = hh_ref[slot - 2, row - rows]
            v = silu((v.astype(F32) - mean) * scale + shift)
            keep = None
            if row < 2:
                keep = tile > 0
            if row >= rows + 2:
                keep = tile < last
            if slot < 2:
                keep = (tm > 0) if keep is None else keep & (tm > 0)
            if keep is not None:
                v = jnp.where(keep, v, 0.0)
            put_both(put_row(v, a_ref, b_ref, slot, row), d_ref, slot, row)

    def join(f, r, out):
        v = out + own_ref[f, r + 2].astype(F32)
        if r == 0:
            v = jnp.where(tile > 0, v, 0.0)
        if r > rows:
            v = jnp.where(tile < last, v, 0.0)
        put_row(v, aj_ref, bj_ref, f, r)

    def joined(runs):
        out = conv_rows(a_ref, b_ref, d_ref, w_ref, runs, cols) + bias
        k = 0
        for f, first, n in runs:
            for r in range(first, first + n):
                join(f, r, out[k * cols : (k + 1) * cols])
                k += 1

    def up_frame(f):
        m = rows * cols
        first = lax.broadcasted_iota(jnp.int32, (m, chan), 1) < chan // 2
        for s in range(2):
            parts = [aj_ref[f, s + i : s + i + rows].reshape(m, 128) for i in range(2)]
            parts.append(bj_ref[f, s : s + rows].reshape(m, 128))
            maps = jnp.concatenate(parts, axis=1)
            sides = jnp.dot(maps, wu_ref[s, 0], preferred_element_type=F32)
            up = jnp.dot(maps, wu_ref[s, 1], preferred_element_type=F32)
            up = up + jnp.where(first, from_left(sides, cols), from_right(sides, cols))
            up = (up + bias_up).astype(BF16).reshape(rows, cols, chan)
            for y in range(rows):
                out_ref[f, 2 * y + s] = up[y]

    for slot in range(4):
        norm_frame(slot)
    written = []
    for f in range(0, frames, 2):
        joined([(f, 1, rows)])
        if f + 4 < frames + 2:
            norm_frame(f + 4)
        joined([(f + 1, 1, rows)])
        if f + 5 < frames + 2:
            norm_frame(f + 5)
        joined([(f + i, r, 1) for i in range(2) for r in (0, rows + 1)])
        for i in range(f, f + 2):
            up_frame(i)
            copy = pltpu.make_async_copy(out_ref.at[i], out_hbm.at[i], out_sems.at[i])
            copy.start()
            written.append(copy)
    for copy in written:
        copy.wait()


def exchange(stat):
    return lax.all_to_all(stat, ("tm", "tile"), 0, 0)


def body(
    features,
    gain_one,
    shift_one,
    kernel_one,
    bias_one,
    gain_two,
    shift_two,
    kernel_two,
    bias_two,
    up_kernel,
    up_bias,
):
    x = features[0]
    frames, rows, cols, chan = x.shape
    tiles = lax.axis_size("tile")
    even_pairs = [(i, i ^ 1) for i in range(tiles)]
    odd_pairs = [(i, i + 1) for i in range(1, tiles - 1, 2)]
    odd_pairs += [(b, a) for a, b in odd_pairs]
    down = [(0, 1)]
    shape = jax.ShapeDtypeStruct
    stat_shape = shape((2 * tiles, 2, 128), F32)
    small = pltpu.CompilerParams(vmem_limit_bytes=12 * 2**20)
    limit = pltpu.CompilerParams(vmem_limit_bytes=LIMIT)
    one_conv = 2 * frames * rows * cols * 27 * chan * chan
    cost = lambda flops, moved: pl.CostEstimate(
        flops=flops, bytes_accessed=moved, transcendentals=0
    )

    even, odd, stat = pl.pallas_call(
        pack_kernel,
        out_shape=(
            shape((frames, 3, cols, chan), BF16),
            shape((frames, 3, cols, chan), BF16),
            stat_shape,
        ),
        in_specs=[VM],
        out_specs=(VM, VM, VM),
        compiler_params=small,
        name="pack",
    )(x)
    p1 = lax.ppermute(even, "tile", even_pairs)
    p2 = lax.ppermute(odd, "tile", odd_pairs)
    all_one = exchange(stat)
    w_one = kernel_one.reshape(27, chan, chan)
    w_two = kernel_two.reshape(27, chan, chan)
    own, last_two = pl.pallas_call(
        assemble_kernel,
        out_shape=(
            shape((frames, rows + 6, cols, chan), BF16),
            shape((2, rows + 6, cols, chan), BF16),
        ),
        in_specs=[VM] * 3,
        out_specs=(VM, VM),
        compiler_params=small,
        name="assemble",
    )(x, p1, p2)
    before = lax.ppermute(last_two, "tm", down)
    row = lambda v: v.reshape(1, v.shape[0])
    parts = [row(v) for v in (shift_one, bias_one, shift_two, bias_two, up_bias)]
    vectors = pl.pallas_call(
        vectors_kernel,
        out_shape=shape((5, chan), F32),
        in_specs=[VM] * 5,
        out_specs=VM,
        compiler_params=small,
        cost_estimate=cost(FILL_FLOPS, 2**14),
        name="vectors",
    )(*parts)

    def table(stats, gain):
        rows_of = shape((8, 1, chan), F32)
        return pl.pallas_call(
            functools.partial(table_kernel, rows * cols * (chan // G)),
            out_shape=(rows_of, rows_of),
            in_specs=[VM, VM],
            out_specs=(VM, VM),
            compiler_params=small,
            cost_estimate=cost(TABLE_FLOPS, 2**18),
            name="table",
        )(stats, gain.reshape(1, chan))

    def scratch(in_rows):
        return [
            pltpu.VMEM((frames + 2, in_rows, cols, 128), BF16),
            pltpu.VMEM((frames + 2, in_rows, cols, 128), BF16),
            pltpu.VMEM((frames, in_rows, cols, 128), BF16),
        ]

    args = (own, before, w_one)
    table_one = table(all_one, gain_one)

    def conv_one(ring, row_list, *more):
        outs = (shape((frames, rows, cols, chan), BF16),)
        outs += (stat_shape,) if ring else (shape((2, rows + 4, cols, chan), BF16),)
        return pl.pallas_call(
            functools.partial(conv_one_kernel, ring, row_list),
            out_shape=outs,
            in_specs=[VM] * (len(args) + 3) + [HB] * len(more),
            out_specs=(VM,) * len(outs),
            scratch_shapes=scratch(sum(n + 2 for _, n, _ in row_list))
            + [pltpu.SemaphoreType.DMA] * len(more),
            compiler_params=limit,
            cost_estimate=cost(one_conv if ring else RIM_FLOPS, 4 * 2**20),
            name="conv_one" if ring else "conv_one_rim",
        )(*args, vectors, *table_one, *more)

    hidden, stat_two = conv_one(True, ((2, rows, 0),))
    all_two = exchange(stat_two)
    rim, hidden_two = conv_one(False, ((0, 2, 0), (rows + 2, 2, 2)), hidden)
    hidden_before = lax.ppermute(hidden_two, "tm", down)
    w_up = pl.pallas_call(
        fold_kernel,
        out_shape=shape((2, 2, 2 * chan, chan), BF16),
        in_specs=[VM, HB],
        out_specs=VM,
        compiler_params=small,
        cost_estimate=cost(FILL_FLOPS, 2 * 2**20),
        name="fold",
    )(up_kernel.reshape(9, chan, chan // 2), stat_two)
    args_two = (own, hidden, rim, hidden_before, w_two, w_up)
    out_shape = shape((frames, 2 * rows, cols, chan), BF16)
    out = pl.pallas_call(
        conv_two_kernel,
        out_shape=out_shape,
        in_specs=[VM] * (len(args_two) + 3),
        out_specs=HB,
        scratch_shapes=[pltpu.VMEM(out_shape.shape, BF16)]
        + scratch(rows + 4)
        + [
            pltpu.VMEM((frames, rows + 2, cols, 128), BF16),
            pltpu.VMEM((frames, rows + 2, cols, 128), BF16),
            pltpu.SemaphoreType.DMA((frames,)),
        ],
        compiler_params=limit,
        cost_estimate=cost(3 * one_conv, 4 * 2**20),
        name="conv_two",
    )(*args_two, vectors, *table(all_two, gain_two))
    return out[None]


def solution(mesh):
    return jax.shard_map(
        body,
        mesh=mesh,
        in_specs=(P(None, "tm", "tile", None, None),) + (P(),) * 10,
        out_specs=P(None, "tm", "tile", None, None),
        check_vma=False,
    )
```

```python
import functools

import jax
import jax.numpy as jnp
from jax import lax
from jax.experimental import pallas as pl
from jax.experimental.pallas import tpu as pltpu
from jax.sharding import PartitionSpec as P

G = 32
EPS = 1e-06
LIMIT = 24 * 2**20
FILL_FLOPS = 15 * 10**9
RIM_FLOPS = 4 * 10**9
TABLE_FLOPS = 1500000000
F32 = jnp.float32
BF16 = jnp.bfloat16
VM = pl.BlockSpec(memory_space=pltpu.VMEM)
HB = pl.BlockSpec(memory_space=pltpu.HBM)


def dot01(a, b):
    high = a.astype(BF16).astype(F32)
    rest = a - high
    middle = rest.astype(BF16).astype(F32)
    parts = jnp.concatenate([high, middle, rest - middle], axis=0).astype(BF16)
    out = jnp.dot(parts, b, preferred_element_type=F32)
    return out[0:8] + out[8:16] + out[16:24]


def spread(chan):
    lane = lax.broadcasted_iota(jnp.int32, (128, chan), 0)
    col = lax.broadcasted_iota(jnp.int32, (128, chan), 1)
    low = (lane & (G - 1)) * (chan // G)
    return jnp.where((col >= low) & (col < low + chan // G), 1.0, 0.0).astype(BF16)


def gather_groups(chan):
    lane = lax.broadcasted_iota(jnp.int32, (chan, 128), 1)
    col = lax.broadcasted_iota(jnp.int32, (chan, 128), 0)
    low = (lane & (G - 1)) * (chan // G)
    return jnp.where((col >= low) & (col < low + chan // G), 1.0, 0.0).astype(BF16)


def frame_mask(first):
    lane = lax.broadcasted_iota(jnp.int32, (8, 128), 1)
    row = lax.broadcasted_iota(jnp.int32, (8, 128), 0)
    low = (row - first) * G
    return (lane >= low) & (lane < low + G)


def stack_rows(rows):
    width = rows[0].shape[1]
    index = lax.broadcasted_iota(jnp.int32, (8, width), 0)
    out = jnp.zeros((8, width), F32)
    for i, r in enumerate(rows):
        out = jnp.where(index == i, jnp.broadcast_to(r, (8, width)), out)
    return out


def channel_stats(v):
    mean = jnp.sum(v, axis=0, keepdims=True) / v.shape[0]
    off = v - mean
    return mean, jnp.sum(off * off, axis=0, keepdims=True)


def local_stats(stats, positions, stat_ref):
    chan = stats[0][0].shape[1]
    mask = frame_mask(0)
    to_group, to_chan = gather_groups(chan), spread(chan)
    means = stack_rows([m for m, _ in stats])
    squares = stack_rows([q for _, q in stats])
    mean = jnp.where(mask, dot01(means, to_group), 0.0) / (chan // G)
    off = means - dot01(mean, to_chan)
    square = jnp.where(mask, dot01(squares + positions * off * off, to_group), 0.0)
    packed = jnp.concatenate(
        [jnp.sum(mean, axis=0, keepdims=True), jnp.sum(square, axis=0, keepdims=True)], axis=0
    )
    stat_ref[...] = jnp.broadcast_to(packed[None], stat_ref.shape)


def table_kernel(count, stat_ref, gain_ref, mean_ref, scale_ref):
    gain = gain_ref[...]
    tiles = stat_ref.shape[0] // 2
    chan = mean_ref.shape[-1]
    to_chan = spread(chan)
    means, spreads = [], []
    for half in range(2):
        part = stat_ref[half * tiles : (half + 1) * tiles]
        total = jnp.sum(part, axis=0)
        mean = total[0:1] / tiles
        off = part - mean[None]
        spread_sum = total[1:2] + count * jnp.sum(off * off, axis=0)[0:1]
        means.append(mean)
        spreads.append(spread_sum / (tiles * count))
    m0, m1 = frame_mask(0), frame_mask(4)
    mean8 = jnp.where(m0, means[0], 0.0) + jnp.where(m1, means[1], 0.0)
    inv8 = jnp.where(m0, lax.rsqrt(spreads[0] + EPS), 0.0) + jnp.where(
        m1, lax.rsqrt(spreads[1] + EPS), 0.0
    )
    mean_chan = dot01(mean8, to_chan)
    scale = dot01(inv8, to_chan) * gain
    for f in range(8):
        mean_ref[f] = mean_chan[f : f + 1]
        scale_ref[f] = scale[f : f + 1]


def columns(shape, cols):
    return lax.broadcasted_iota(jnp.int32, shape, 0) & (cols - 1)


def from_left(v, cols):
    return jnp.where(columns(v.shape, cols) == 0, 0.0, pltpu.roll(v, 1, axis=0))


def from_right(v, cols):
    turned = pltpu.roll(v, v.shape[0] - 1, axis=0)
    return jnp.where(columns(v.shape, cols) == cols - 1, 0.0, turned)


def put_row(v, a_ref, b_ref, f, k):
    tail = v[:, 128:192].astype(BF16)
    a_ref[f, k] = v[:, 0:128].astype(BF16)
    b_ref[f, k, :, 0:64] = tail
    if k > 0:
        b_ref[f, k - 1, :, 64:128] = tail
    return tail


def silu(u):
    half = 0.5 * u
    return half + half * jnp.tanh(half)


def conv_rows(a_ref, b_ref, d_ref, w_ref, runs, cols):
    def take(ref, t, r):
        parts = [ref[f + t, k + r : k + r + n].reshape(n * cols, 128) for f, k, n in runs]
        return parts[0] if len(parts) == 1 else jnp.concatenate(parts, axis=0)

    parts = [take(a_ref, t, r) for t in range(3) for r in range(3)]
    parts += [take(b_ref, t, 0) for t in range(3)]
    parts += [take(d_ref, 0, 2), take(b_ref, 2, 2)]
    maps = jnp.concatenate(parts, axis=1)

    def taps(k):
        low, high = slice(0, 128), slice(128, 192)
        at = lambda t, r: (t * 3 + r) * 3 + k
        rows = [w_ref[at(t, r), low] for t in range(3) for r in range(3)]
        for t in range(3):
            rows += [w_ref[at(t, 0), high], w_ref[at(t, 1), high]]
        rows += [w_ref[at(0, 2), high], w_ref[at(1, 2), high], w_ref[at(2, 2), high]]
        rows.append(jnp.zeros((64, w_ref.shape[-1]), BF16))
        return jnp.concatenate(rows, axis=0)

    left, centre, right = [
        jnp.dot(maps, taps(k), preferred_element_type=F32) for k in range(3)
    ]
    return centre + from_left(left, cols) + from_right(right, cols)


def pack_kernel(x_ref, even_ref, odd_ref, stat_ref):
    odd = lax.rem(lax.axis_index("tile"), 2)
    frames, rows, cols, chan = x_ref.shape
    even_ref[...] = x_ref[:, pl.ds(1 - odd, 3)]
    odd_ref[...] = x_ref[:, pl.ds(odd, 3)]
    stats = [
        channel_stats(x_ref[f].reshape(rows * cols, chan).astype(F32)) for f in range(frames)
    ]
    local_stats(stats, rows * cols, stat_ref)


def assemble_kernel(x_ref, p1_ref, p2_ref, own_ref, c_ref):
    frames, rows = x_ref.shape[:2]
    odd = lax.rem(lax.axis_index("tile"), 2) == 1
    for f in range(frames):
        for r in range(3):
            p1, p2 = p1_ref[f, r].astype(F32), p2_ref[f, r].astype(F32)
            own_ref[f, r] = jnp.where(odd, p1, p2).astype(BF16)
            own_ref[f, 3 + rows + r] = jnp.where(odd, p2, p1).astype(BF16)
    own_ref[:, 3 : 3 + rows] = x_ref[...]
    c_ref[...] = own_ref[frames - 2 :]


def vectors_kernel(*refs):
    for i, ref in enumerate(refs[:-1]):
        refs[-1][i : i + 1, 0 : ref.shape[1]] = ref[...]
    half = refs[-2].shape[1]
    refs[-1][len(refs) - 2 : len(refs) - 1, half : 2 * half] = refs[-2][...]


def fold_kernel(k_ref, after_hbm, wu_ref):
    k = [[k_ref[3 * j + i].astype(F32) for i in range(3)] for j in range(3)]
    plus = lambda p, q: [a + b for a, b in zip(p, q)]
    for s, taps in enumerate(((k[0], plus(k[1], k[2])), (plus(k[0], k[1]), k[2]))):
        for i, c in enumerate(taps):
            sides = jnp.concatenate([c[0], c[2]], axis=1).astype(BF16)
            centre = jnp.concatenate([c[1] + c[2], c[0] + c[1]], axis=1).astype(BF16)
            for j, v in enumerate((sides, centre)):
                wu_ref[s, j, 128 * i : 128 * i + 128] = v[:128]
                wu_ref[s, j, 256 + 64 * i : 320 + 64 * i] = v[128:]


def conv_one_kernel(
    ring, row_list, own_ref, c_ref, w_ref, vec_ref, mean_ref, scale_ref, *rest
):
    if ring:
        out_hbm, stat_ref, a_ref, b_ref, d_ref, out_ref, out_sems = rest
    else:
        h_hbm, out_hbm, cache_ref, a_ref, b_ref, d_ref, out_ref, out_sems, sem = rest
    frames, rows, cols, chan = own_ref.shape
    rows -= 6
    if not ring:
        load_h = pltpu.make_async_copy(
            h_hbm.at[pl.ds(frames - 2, 2)], cache_ref.at[:, pl.ds(2, rows)], sem
        )
        load_h.start()
    tm, tile = lax.axis_index("tm"), lax.axis_index("tile")
    last = lax.axis_size("tile") - 1
    shift, bias = vec_ref[0:1], vec_ref[1:2]
    in_rows = a_ref.shape[1]
    b_ref[:, in_rows - 1] = jnp.zeros_like(b_ref[:, in_rows - 1])

    def fetch(slot, row):
        v = c_ref[slot, row] if slot < 2 else own_ref[slot - 2, row]
        return v.astype(F32)

    def norm_frame(slot):
        index = slot + frames - 2 if slot < 2 else tm * frames + slot - 2
        mean, scale = mean_ref[index], scale_ref[index]
        k = 0
        for first, n, _ in row_list:
            for row in range(first, first + n + 2):
                v = silu((fetch(slot, row) - mean) * scale + shift)
                keep = None
                if row < 3:
                    keep = tile > 0
                if row >= 3 + rows:
                    keep = tile < last
                if slot < 2:
                    keep = (tm > 0) if keep is None else keep & (tm > 0)
                if keep is not None:
                    v = jnp.where(keep, v, 0.0)
                put_both(put_row(v, a_ref, b_ref, slot, k), d_ref, slot, k)
                k += 1

    norm_frame(0)
    norm_frame(1)
    stats, written, runs, k = [], [], [], 0
    for _, n, _ in row_list:
        runs.append((k, n))
        k += n + 2
    for f in range(frames):
        norm_frame(f + 2)
        here = [(f, first, n) for first, n in runs]
        out = (conv_rows(a_ref, b_ref, d_ref, w_ref, here, cols) + bias).astype(BF16)
        rows_out = out.reshape(rows, cols, chan)
        k = 0
        for _, n, where_to in row_list:
            out_ref[f, where_to : where_to + n] = rows_out[k : k + n]
            if not ring and f >= frames - 2:
                at = where_to if where_to == 0 else where_to + rows
                cache_ref[f - frames + 2, at : at + n] = rows_out[k : k + n]
            k += n
        copy = pltpu.make_async_copy(out_ref.at[f], out_hbm.at[f], out_sems.at[f])
        copy.start()
        written.append(copy)
        if ring:
            stats.append(channel_stats(out.astype(F32)))
    if ring:
        local_stats(stats, rows * cols, stat_ref)
    else:
        load_h.wait()
    for copy in written:
        copy.wait()


def put_both(tail, d_ref, slot, k):
    if slot < d_ref.shape[0]:
        d_ref[slot, k, :, 0:64] = tail
    if 0 < slot <= d_ref.shape[0]:
        d_ref[slot - 1, k, :, 64:128] = tail


def conv_two_kernel(
    own_ref,
    h_ref,
    hh_ref,
    hc_ref,
    w_ref,
    wu_ref,
    vec_ref,
    mean_ref,
    scale_ref,
    out_hbm,
    out_ref,
    a_ref,
    b_ref,
    d_ref,
    aj_ref,
    bj_ref,
    out_sems,
):
    frames, rows, cols, chan = h_ref.shape
    tm, tile = lax.axis_index("tm"), lax.axis_index("tile")
    last = lax.axis_size("tile") - 1
    shift, bias, bias_up = vec_ref[2:3], vec_ref[3:4], vec_ref[4:5]
    in_rows = a_ref.shape[1]
    b_ref[:, in_rows - 1] = jnp.zeros_like(b_ref[:, in_rows - 1])

    def norm_frame(slot):
        index = slot + frames - 2 if slot < 2 else tm * frames + slot - 2
        mean, scale = mean_ref[index], scale_ref[index]
        for row in range(rows + 4):
            if slot < 2:
                v = hc_ref[slot, row]
            elif row < 2:
                v = hh_ref[slot - 2, row]
            elif row < rows + 2:
                v = h_ref[slot - 2, row - 2]
            else:
                v = hh_ref[slot - 2, row - rows]
            v = silu((v.astype(F32) - mean) * scale + shift)
            keep = None
            if row < 2:
                keep = tile > 0
            if row >= rows + 2:
                keep = tile < last
            if slot < 2:
                keep = (tm > 0) if keep is None else keep & (tm > 0)
            if keep is not None:
                v = jnp.where(keep, v, 0.0)
            put_both(put_row(v, a_ref, b_ref, slot, row), d_ref, slot, row)

    def join(f, r, out):
        v = out + own_ref[f, r + 2].astype(F32)
        if r == 0:
            v = jnp.where(tile > 0, v, 0.0)
        if r > rows:
            v = jnp.where(tile < last, v, 0.0)
        put_row(v, aj_ref, bj_ref, f, r)

    def joined(runs):
        out = conv_rows(a_ref, b_ref, d_ref, w_ref, runs, cols) + bias
        k = 0
        for f, first, n in runs:
            for r in range(first, first + n):
                join(f, r, out[k * cols : (k + 1) * cols])
                k += 1

    def up_frame(f):
        m = rows * cols
        first = lax.broadcasted_iota(jnp.int32, (m, chan), 1) < chan // 2
        for s in range(2):
            parts = [aj_ref[f, s + i : s + i + rows].reshape(m, 128) for i in range(2)]
            parts.append(bj_ref[f, s : s + rows].reshape(m, 128))
            maps = jnp.concatenate(parts, axis=1)
            sides = jnp.dot(maps, wu_ref[s, 0], preferred_element_type=F32)
            up = jnp.dot(maps, wu_ref[s, 1], preferred_element_type=F32)
            up = up + jnp.where(first, from_left(sides, cols), from_right(sides, cols))
            up = (up + bias_up).astype(BF16).reshape(rows, cols, chan)
            for y in range(rows):
                out_ref[f, 2 * y + s] = up[y]

    for slot in range(4):
        norm_frame(slot)
    written = []
    for f in range(0, frames, 2):
        joined([(f, 1, rows)])
        if f + 4 < frames + 2:
            norm_frame(f + 4)
        joined([(f + 1, 1, rows)])
        if f + 5 < frames + 2:
            norm_frame(f + 5)
        joined([(f + i, r, 1) for i in range(2) for r in (0, rows + 1)])
        for i in range(f, f + 2):
            up_frame(i)
            copy = pltpu.make_async_copy(out_ref.at[i], out_hbm.at[i], out_sems.at[i])
            copy.start()
            written.append(copy)
    for copy in written:
        copy.wait()


def exchange(stat):
    return lax.all_to_all(stat, ("tm", "tile"), 0, 0)


def body(
    features,
    gain_one,
    shift_one,
    kernel_one,
    bias_one,
    gain_two,
    shift_two,
    kernel_two,
    bias_two,
    up_kernel,
    up_bias,
):
    x = features[0]
    frames, rows, cols, chan = x.shape
    tiles = lax.axis_size("tile")
    even_pairs = [(i, i ^ 1) for i in range(tiles)]
    odd_pairs = [(i, i + 1) for i in range(1, tiles - 1, 2)]
    odd_pairs += [(b, a) for a, b in odd_pairs]
    down = [(0, 1)]
    shape = jax.ShapeDtypeStruct
    stat_shape = shape((2 * tiles, 2, 128), F32)
    small = pltpu.CompilerParams(vmem_limit_bytes=12 * 2**20)
    limit = pltpu.CompilerParams(vmem_limit_bytes=LIMIT)
    one_conv = 2 * frames * rows * cols * 27 * chan * chan
    cost = lambda flops, moved: pl.CostEstimate(
        flops=flops, bytes_accessed=moved, transcendentals=0
    )

    even, odd, stat = pl.pallas_call(
        pack_kernel,
        out_shape=(
            shape((frames, 3, cols, chan), BF16),
            shape((frames, 3, cols, chan), BF16),
            stat_shape,
        ),
        in_specs=[VM],
        out_specs=(VM, VM, VM),
        compiler_params=small,
        name="pack",
    )(x)
    p1 = lax.ppermute(even, "tile", even_pairs)
    p2 = lax.ppermute(odd, "tile", odd_pairs)
    all_one = exchange(stat)
    w_one = kernel_one.reshape(27, chan, chan)
    w_two = kernel_two.reshape(27, chan, chan)
    own, last_two = pl.pallas_call(
        assemble_kernel,
        out_shape=(
            shape((frames, rows + 6, cols, chan), BF16),
            shape((2, rows + 6, cols, chan), BF16),
        ),
        in_specs=[VM] * 3,
        out_specs=(VM, VM),
        compiler_params=small,
        name="assemble",
    )(x, p1, p2)
    before = lax.ppermute(last_two, "tm", down)
    row = lambda v: v.reshape(1, v.shape[0])
    parts = [row(v) for v in (shift_one, bias_one, shift_two, bias_two, up_bias)]
    vectors = pl.pallas_call(
        vectors_kernel,
        out_shape=shape((5, chan), F32),
        in_specs=[VM] * 5,
        out_specs=VM,
        compiler_params=small,
        cost_estimate=cost(FILL_FLOPS, 2**14),
        name="vectors",
    )(*parts)

    def table(stats, gain):
        rows_of = shape((8, 1, chan), F32)
        return pl.pallas_call(
            functools.partial(table_kernel, rows * cols * (chan // G)),
            out_shape=(rows_of, rows_of),
            in_specs=[VM, VM],
            out_specs=(VM, VM),
            compiler_params=small,
            cost_estimate=cost(TABLE_FLOPS, 2**18),
            name="table",
        )(stats, gain.reshape(1, chan))

    def scratch(in_rows):
        return [
            pltpu.VMEM((frames + 2, in_rows, cols, 128), BF16),
            pltpu.VMEM((frames + 2, in_rows, cols, 128), BF16),
            pltpu.VMEM((frames, in_rows, cols, 128), BF16),
        ]

    args = (own, before, w_one)
    table_one = table(all_one, gain_one)

    def conv_one(ring, row_list, *more):
        outs = (pltpu.HBM((frames, rows, cols, chan), BF16),)
        extra = [
            pltpu.VMEM((frames, rows, cols, chan), BF16),
            pltpu.SemaphoreType.DMA((frames,)),
        ] + [pltpu.SemaphoreType.DMA] * len(more)
        outs += (stat_shape,) if ring else (shape((2, rows + 4, cols, chan), BF16),)
        return pl.pallas_call(
            functools.partial(conv_one_kernel, ring, row_list),
            out_shape=outs,
            in_specs=[VM] * (len(args) + 3) + [HB] * len(more),
            out_specs=(HB, VM),
            scratch_shapes=scratch(sum(n + 2 for _, n, _ in row_list)) + extra,
            compiler_params=limit,
            cost_estimate=cost(one_conv if ring else RIM_FLOPS, 4 * 2**20),
            name="conv_one" if ring else "conv_one_rim",
        )(*args, vectors, *table_one, *more)

    hidden, stat_two = conv_one(True, ((2, rows, 0),))
    all_two = exchange(stat_two)
    rim, hidden_two = conv_one(False, ((0, 2, 0), (rows + 2, 2, 2)), hidden)
    hidden_before = lax.ppermute(hidden_two, "tm", down)
    w_up = pl.pallas_call(
        fold_kernel,
        out_shape=shape((2, 2, 2 * chan, chan), BF16),
        in_specs=[VM, HB],
        out_specs=VM,
        compiler_params=small,
        cost_estimate=cost(FILL_FLOPS, 2 * 2**20),
        name="fold",
    )(up_kernel.reshape(9, chan, chan // 2), stat_two)
    args_two = (own, hidden, rim, hidden_before, w_two, w_up)
    out_shape = shape((frames, 2 * rows, cols, chan), BF16)
    out = pl.pallas_call(
        conv_two_kernel,
        out_shape=out_shape,
        in_specs=[VM] * (len(args_two) + 3),
        out_specs=HB,
        scratch_shapes=[pltpu.VMEM(out_shape.shape, BF16)]
        + scratch(rows + 4)
        + [
            pltpu.VMEM((frames, rows + 2, cols, 128), BF16),
            pltpu.VMEM((frames, rows + 2, cols, 128), BF16),
            pltpu.SemaphoreType.DMA((frames,)),
        ],
        compiler_params=limit,
        cost_estimate=cost(3 * one_conv, 4 * 2**20),
        name="conv_two",
    )(*args_two, vectors, *table(all_two, gain_two))
    return out[None]


def solution(mesh):
    return jax.shard_map(
        body,
        mesh=mesh,
        in_specs=(P(None, "tm", "tile", None, None),) + (P(),) * 10,
        out_specs=P(None, "tm", "tile", None, None),
        check_vma=False,
    )
```

```python
import functools

import jax
import jax.numpy as jnp
from jax import lax
from jax.experimental import pallas as pl
from jax.experimental.pallas import tpu as pltpu
from jax.sharding import PartitionSpec as P

G = 32
EPS = 1e-06
LIMIT = 24 * 2**20
FILL_FLOPS = 15 * 10**9
RIM_FLOPS = 4 * 10**9
TABLE_FLOPS = 1500000000
F32 = jnp.float32
BF16 = jnp.bfloat16
VM = pl.BlockSpec(memory_space=pltpu.VMEM)
HB = pl.BlockSpec(memory_space=pltpu.HBM)


def dot01(a, b):
    high = a.astype(BF16).astype(F32)
    rest = a - high
    middle = rest.astype(BF16).astype(F32)
    parts = jnp.concatenate([high, middle, rest - middle], axis=0).astype(BF16)
    out = jnp.dot(parts, b, preferred_element_type=F32)
    return out[0:8] + out[8:16] + out[16:24]


def spread(chan):
    lane = lax.broadcasted_iota(jnp.int32, (128, chan), 0)
    col = lax.broadcasted_iota(jnp.int32, (128, chan), 1)
    low = (lane & (G - 1)) * (chan // G)
    return jnp.where((col >= low) & (col < low + chan // G), 1.0, 0.0).astype(BF16)


def gather_groups(chan):
    lane = lax.broadcasted_iota(jnp.int32, (chan, 128), 1)
    col = lax.broadcasted_iota(jnp.int32, (chan, 128), 0)
    low = (lane & (G - 1)) * (chan // G)
    return jnp.where((col >= low) & (col < low + chan // G), 1.0, 0.0).astype(BF16)


def frame_mask(first):
    lane = lax.broadcasted_iota(jnp.int32, (8, 128), 1)
    row = lax.broadcasted_iota(jnp.int32, (8, 128), 0)
    low = (row - first) * G
    return (lane >= low) & (lane < low + G)


def stack_rows(rows):
    width = rows[0].shape[1]
    index = lax.broadcasted_iota(jnp.int32, (8, width), 0)
    out = jnp.zeros((8, width), F32)
    for i, r in enumerate(rows):
        out = jnp.where(index == i, jnp.broadcast_to(r, (8, width)), out)
    return out


def channel_stats(v):
    mean = jnp.sum(v, axis=0, keepdims=True) / v.shape[0]
    off = v - mean
    return mean, jnp.sum(off * off, axis=0, keepdims=True)


def local_stats(stats, positions, stat_ref):
    chan = stats[0][0].shape[1]
    mask = frame_mask(0)
    to_group, to_chan = gather_groups(chan), spread(chan)
    means = stack_rows([m for m, _ in stats])
    squares = stack_rows([q for _, q in stats])
    mean = jnp.where(mask, dot01(means, to_group), 0.0) / (chan // G)
    off = means - dot01(mean, to_chan)
    square = jnp.where(mask, dot01(squares + positions * off * off, to_group), 0.0)
    packed = jnp.concatenate(
        [jnp.sum(mean, axis=0, keepdims=True), jnp.sum(square, axis=0, keepdims=True)], axis=0
    )
    stat_ref[...] = jnp.broadcast_to(packed[None], stat_ref.shape)


def table_kernel(count, stat_ref, gain_ref, mean_ref, scale_ref):
    gain = gain_ref[...]
    tiles = stat_ref.shape[0] // 2
    chan = mean_ref.shape[-1]
    to_chan = spread(chan)
    means, spreads = [], []
    for half in range(2):
        part = stat_ref[half * tiles : (half + 1) * tiles]
        total = jnp.sum(part, axis=0)
        mean = total[0:1] / tiles
        off = part - mean[None]
        spread_sum = total[1:2] + count * jnp.sum(off * off, axis=0)[0:1]
        means.append(mean)
        spreads.append(spread_sum / (tiles * count))
    m0, m1 = frame_mask(0), frame_mask(4)
    mean8 = jnp.where(m0, means[0], 0.0) + jnp.where(m1, means[1], 0.0)
    inv8 = jnp.where(m0, lax.rsqrt(spreads[0] + EPS), 0.0) + jnp.where(
        m1, lax.rsqrt(spreads[1] + EPS), 0.0
    )
    mean_chan = dot01(mean8, to_chan)
    scale = dot01(inv8, to_chan) * gain
    for f in range(8):
        mean_ref[f] = mean_chan[f : f + 1]
        scale_ref[f] = scale[f : f + 1]


def columns(shape, cols):
    return lax.broadcasted_iota(jnp.int32, shape, 0) & (cols - 1)


def from_left(v, cols):
    return jnp.where(columns(v.shape, cols) == 0, 0.0, pltpu.roll(v, 1, axis=0))


def from_right(v, cols):
    turned = pltpu.roll(v, v.shape[0] - 1, axis=0)
    return jnp.where(columns(v.shape, cols) == cols - 1, 0.0, turned)


def put_row(v, a_ref, b_ref, f, k):
    tail = v[:, 128:192].astype(BF16)
    a_ref[f, k] = v[:, 0:128].astype(BF16)
    b_ref[f, k, :, 0:64] = tail
    if k > 0:
        b_ref[f, k - 1, :, 64:128] = tail
    return tail


def silu(u):
    half = 0.5 * u
    return half + half * jnp.tanh(half)


def conv_rows(a_ref, b_ref, d_ref, w_ref, runs, cols):
    def take(ref, t, r):
        parts = [ref[f + t, k + r : k + r + n].reshape(n * cols, 128) for f, k, n in runs]
        return parts[0] if len(parts) == 1 else jnp.concatenate(parts, axis=0)

    parts = [take(a_ref, t, r) for t in range(3) for r in range(3)]
    parts += [take(b_ref, t, 0) for t in range(3)]
    parts += [take(d_ref, 0, 2), take(b_ref, 2, 2)]
    maps = jnp.concatenate(parts, axis=1)

    def taps(k):
        low, high = slice(0, 128), slice(128, 192)
        at = lambda t, r: (t * 3 + r) * 3 + k
        rows = [w_ref[at(t, r), low] for t in range(3) for r in range(3)]
        for t in range(3):
            rows += [w_ref[at(t, 0), high], w_ref[at(t, 1), high]]
        rows += [w_ref[at(0, 2), high], w_ref[at(1, 2), high], w_ref[at(2, 2), high]]
        rows.append(jnp.zeros((64, w_ref.shape[-1]), BF16))
        return jnp.concatenate(rows, axis=0)

    left, centre, right = [
        jnp.dot(maps, taps(k), preferred_element_type=F32) for k in range(3)
    ]
    return centre + from_left(left, cols) + from_right(right, cols)


def pack_kernel(x_ref, even_ref, odd_ref, stat_ref):
    odd = lax.rem(lax.axis_index("tile"), 2)
    frames, rows, cols, chan = x_ref.shape
    even_ref[...] = x_ref[:, pl.ds(1 - odd, 3)]
    odd_ref[...] = x_ref[:, pl.ds(odd, 3)]
    stats = [
        channel_stats(x_ref[f].reshape(rows * cols, chan).astype(F32)) for f in range(frames)
    ]
    local_stats(stats, rows * cols, stat_ref)


def assemble_kernel(x_ref, p1_ref, p2_ref, own_ref, c_ref):
    frames, rows = x_ref.shape[:2]
    odd = lax.rem(lax.axis_index("tile"), 2) == 1
    for f in range(frames):
        for r in range(3):
            p1, p2 = p1_ref[f, r].astype(F32), p2_ref[f, r].astype(F32)
            own_ref[f, r] = jnp.where(odd, p1, p2).astype(BF16)
            own_ref[f, 3 + rows + r] = jnp.where(odd, p2, p1).astype(BF16)
    own_ref[:, 3 : 3 + rows] = x_ref[...]
    c_ref[...] = own_ref[frames - 2 :]


def vectors_kernel(*refs):
    for i, ref in enumerate(refs[:-1]):
        refs[-1][i : i + 1, 0 : ref.shape[1]] = ref[...]
    half = refs[-2].shape[1]
    refs[-1][len(refs) - 2 : len(refs) - 1, half : 2 * half] = refs[-2][...]


def fold_kernel(k_ref, after_hbm, wu_ref):
    k = [[k_ref[3 * j + i].astype(F32) for i in range(3)] for j in range(3)]
    plus = lambda p, q: [a + b for a, b in zip(p, q)]
    for s, taps in enumerate(((k[0], plus(k[1], k[2])), (plus(k[0], k[1]), k[2]))):
        for i, c in enumerate(taps):
            sides = jnp.concatenate([c[0], c[2]], axis=1).astype(BF16)
            centre = jnp.concatenate([c[1] + c[2], c[0] + c[1]], axis=1).astype(BF16)
            for j, v in enumerate((sides, centre)):
                wu_ref[s, j, 128 * i : 128 * i + 128] = v[:128]
                wu_ref[s, j, 256 + 64 * i : 320 + 64 * i] = v[128:]


def conv_one_kernel(
    ring, row_list, own_ref, c_hbm, w_ref, vec_ref, mean_ref, scale_ref, *rest
):
    c_ref, c_sem = rest[-2:]
    rest = rest[:-2]
    load_c = pltpu.make_async_copy(c_hbm, c_ref, c_sem)
    load_c.start()
    if ring:
        out_hbm, stat_ref, a_ref, b_ref, d_ref, out_ref, out_sems = rest
    else:
        h_hbm, out_hbm, cache_ref, a_ref, b_ref, d_ref, out_ref, out_sems, sem = rest
    frames, rows, cols, chan = own_ref.shape
    rows -= 6
    if not ring:
        load_h = pltpu.make_async_copy(
            h_hbm.at[pl.ds(frames - 2, 2)], cache_ref.at[:, pl.ds(2, rows)], sem
        )
        load_h.start()
    tm, tile = lax.axis_index("tm"), lax.axis_index("tile")
    last = lax.axis_size("tile") - 1
    shift, bias = vec_ref[0:1], vec_ref[1:2]
    in_rows = a_ref.shape[1]
    b_ref[:, in_rows - 1] = jnp.zeros_like(b_ref[:, in_rows - 1])

    def fetch(slot, row):
        v = c_ref[slot, row] if slot < 2 else own_ref[slot - 2, row]
        return v.astype(F32)

    def norm_frame(slot):
        index = slot + frames - 2 if slot < 2 else tm * frames + slot - 2
        mean, scale = mean_ref[index], scale_ref[index]
        k = 0
        for first, n, _ in row_list:
            for row in range(first, first + n + 2):
                v = silu((fetch(slot, row) - mean) * scale + shift)
                keep = None
                if row < 3:
                    keep = tile > 0
                if row >= 3 + rows:
                    keep = tile < last
                if slot < 2:
                    keep = (tm > 0) if keep is None else keep & (tm > 0)
                if keep is not None:
                    v = jnp.where(keep, v, 0.0)
                put_both(put_row(v, a_ref, b_ref, slot, k), d_ref, slot, k)
                k += 1

    norm_frame(2)
    load_c.wait()
    norm_frame(0)
    norm_frame(1)
    stats, written, runs, k = [], [], [], 0
    for _, n, _ in row_list:
        runs.append((k, n))
        k += n + 2
    for f in range(frames):
        if f > 0:
            norm_frame(f + 2)
        here = [(f, first, n) for first, n in runs]
        out = (conv_rows(a_ref, b_ref, d_ref, w_ref, here, cols) + bias).astype(BF16)
        rows_out = out.reshape(rows, cols, chan)
        k = 0
        for _, n, where_to in row_list:
            out_ref[f, where_to : where_to + n] = rows_out[k : k + n]
            if not ring and f >= frames - 2:
                at = where_to if where_to == 0 else where_to + rows
                cache_ref[f - frames + 2, at : at + n] = rows_out[k : k + n]
            k += n
        copy = pltpu.make_async_copy(out_ref.at[f], out_hbm.at[f], out_sems.at[f])
        copy.start()
        written.append(copy)
        if ring:
            stats.append(channel_stats(out.astype(F32)))
    if ring:
        local_stats(stats, rows * cols, stat_ref)
    else:
        load_h.wait()
    for copy in written:
        copy.wait()


def put_both(tail, d_ref, slot, k):
    if slot < d_ref.shape[0]:
        d_ref[slot, k, :, 0:64] = tail
    if 0 < slot <= d_ref.shape[0]:
        d_ref[slot - 1, k, :, 64:128] = tail


def conv_two_kernel(
    own_ref,
    h_ref,
    hh_ref,
    hc_ref,
    w_ref,
    wu_ref,
    vec_ref,
    mean_ref,
    scale_ref,
    out_hbm,
    out_ref,
    a_ref,
    b_ref,
    d_ref,
    aj_ref,
    bj_ref,
    out_sems,
):
    frames, rows, cols, chan = h_ref.shape
    tm, tile = lax.axis_index("tm"), lax.axis_index("tile")
    last = lax.axis_size("tile") - 1
    shift, bias, bias_up = vec_ref[2:3], vec_ref[3:4], vec_ref[4:5]
    in_rows = a_ref.shape[1]
    b_ref[:, in_rows - 1] = jnp.zeros_like(b_ref[:, in_rows - 1])

    def norm_frame(slot):
        index = slot + frames - 2 if slot < 2 else tm * frames + slot - 2
        mean, scale = mean_ref[index], scale_ref[index]
        for row in range(rows + 4):
            if slot < 2:
                v = hc_ref[slot, row]
            elif row < 2:
                v = hh_ref[slot - 2, row]
            elif row < rows + 2:
                v = h_ref[slot - 2, row - 2]
            else:
                v = hh_ref[slot - 2, row - rows]
            v = silu((v.astype(F32) - mean) * scale + shift)
            keep = None
            if row < 2:
                keep = tile > 0
            if row >= rows + 2:
                keep = tile < last
            if slot < 2:
                keep = (tm > 0) if keep is None else keep & (tm > 0)
            if keep is not None:
                v = jnp.where(keep, v, 0.0)
            put_both(put_row(v, a_ref, b_ref, slot, row), d_ref, slot, row)

    def join(f, r, out):
        v = out + own_ref[f, r + 2].astype(F32)
        if r == 0:
            v = jnp.where(tile > 0, v, 0.0)
        if r > rows:
            v = jnp.where(tile < last, v, 0.0)
        put_row(v, aj_ref, bj_ref, f, r)

    def joined(runs):
        out = conv_rows(a_ref, b_ref, d_ref, w_ref, runs, cols) + bias
        k = 0
        for f, first, n in runs:
            for r in range(first, first + n):
                join(f, r, out[k * cols : (k + 1) * cols])
                k += 1

    def up_frame(f):
        m = rows * cols
        first = lax.broadcasted_iota(jnp.int32, (m, chan), 1) < chan // 2
        for s in range(2):
            parts = [aj_ref[f, s + i : s + i + rows].reshape(m, 128) for i in range(2)]
            parts.append(bj_ref[f, s : s + rows].reshape(m, 128))
            maps = jnp.concatenate(parts, axis=1)
            sides = jnp.dot(maps, wu_ref[s, 0], preferred_element_type=F32)
            up = jnp.dot(maps, wu_ref[s, 1], preferred_element_type=F32)
            up = up + jnp.where(first, from_left(sides, cols), from_right(sides, cols))
            up = (up + bias_up).astype(BF16).reshape(rows, cols, chan)
            for y in range(rows):
                out_ref[f, 2 * y + s] = up[y]

    for slot in range(4):
        norm_frame(slot)
    written = []
    for f in range(0, frames, 2):
        joined([(f, 1, rows)])
        if f + 4 < frames + 2:
            norm_frame(f + 4)
        joined([(f + 1, 1, rows)])
        if f + 5 < frames + 2:
            norm_frame(f + 5)
        joined([(f + i, r, 1) for i in range(2) for r in (0, rows + 1)])
        for i in range(f, f + 2):
            up_frame(i)
            copy = pltpu.make_async_copy(out_ref.at[i], out_hbm.at[i], out_sems.at[i])
            copy.start()
            written.append(copy)
    for copy in written:
        copy.wait()


def exchange(stat):
    return lax.all_to_all(stat, ("tm", "tile"), 0, 0)


def body(
    features,
    gain_one,
    shift_one,
    kernel_one,
    bias_one,
    gain_two,
    shift_two,
    kernel_two,
    bias_two,
    up_kernel,
    up_bias,
):
    x = features[0]
    frames, rows, cols, chan = x.shape
    tiles = lax.axis_size("tile")
    even_pairs = [(i, i ^ 1) for i in range(tiles)]
    odd_pairs = [(i, i + 1) for i in range(1, tiles - 1, 2)]
    odd_pairs += [(b, a) for a, b in odd_pairs]
    down = [(0, 1)]
    shape = jax.ShapeDtypeStruct
    stat_shape = shape((2 * tiles, 2, 128), F32)
    small = pltpu.CompilerParams(vmem_limit_bytes=12 * 2**20)
    limit = pltpu.CompilerParams(vmem_limit_bytes=LIMIT)
    one_conv = 2 * frames * rows * cols * 27 * chan * chan
    cost = lambda flops, moved: pl.CostEstimate(
        flops=flops, bytes_accessed=moved, transcendentals=0
    )

    even, odd, stat = pl.pallas_call(
        pack_kernel,
        out_shape=(
            shape((frames, 3, cols, chan), BF16),
            shape((frames, 3, cols, chan), BF16),
            stat_shape,
        ),
        in_specs=[VM],
        out_specs=(VM, VM, VM),
        compiler_params=small,
        name="pack",
    )(x)
    p1 = lax.ppermute(even, "tile", even_pairs)
    p2 = lax.ppermute(odd, "tile", odd_pairs)
    all_one = exchange(stat)
    w_one = kernel_one.reshape(27, chan, chan)
    w_two = kernel_two.reshape(27, chan, chan)
    own, last_two = pl.pallas_call(
        assemble_kernel,
        out_shape=(
            shape((frames, rows + 6, cols, chan), BF16),
            shape((2, rows + 6, cols, chan), BF16),
        ),
        in_specs=[VM] * 3,
        out_specs=(VM, VM),
        compiler_params=small,
        name="assemble",
    )(x, p1, p2)
    before = lax.ppermute(last_two, "tm", down)
    row = lambda v: v.reshape(1, v.shape[0])
    parts = [row(v) for v in (shift_one, bias_one, shift_two, bias_two, up_bias)]
    vectors = pl.pallas_call(
        vectors_kernel,
        out_shape=shape((5, chan), F32),
        in_specs=[VM] * 5,
        out_specs=VM,
        compiler_params=small,
        cost_estimate=cost(FILL_FLOPS, 2**14),
        name="vectors",
    )(*parts)

    def table(stats, gain):
        rows_of = shape((8, 1, chan), F32)
        return pl.pallas_call(
            functools.partial(table_kernel, rows * cols * (chan // G)),
            out_shape=(rows_of, rows_of),
            in_specs=[VM, VM],
            out_specs=(VM, VM),
            compiler_params=small,
            cost_estimate=cost(TABLE_FLOPS, 2**18),
            name="table",
        )(stats, gain.reshape(1, chan))

    def scratch(in_rows):
        return [
            pltpu.VMEM((frames + 2, in_rows, cols, 128), BF16),
            pltpu.VMEM((frames + 2, in_rows, cols, 128), BF16),
            pltpu.VMEM((frames, in_rows, cols, 128), BF16),
        ]

    args = (own, before, w_one)
    table_one = table(all_one, gain_one)

    def conv_one(ring, row_list, *more):
        outs = (pltpu.HBM((frames, rows, cols, chan), BF16),)
        extra = [
            pltpu.VMEM((frames, rows, cols, chan), BF16),
            pltpu.SemaphoreType.DMA((frames,)),
        ] + [pltpu.SemaphoreType.DMA] * len(more)
        extra += [pltpu.VMEM(before.shape, BF16), pltpu.SemaphoreType.DMA]
        outs += (stat_shape,) if ring else (shape((2, rows + 4, cols, chan), BF16),)
        return pl.pallas_call(
            functools.partial(conv_one_kernel, ring, row_list),
            out_shape=outs,
            in_specs=[VM, HB] + [VM] * 4 + [HB] * len(more),
            out_specs=(HB, VM),
            scratch_shapes=scratch(sum(n + 2 for _, n, _ in row_list)) + extra,
            compiler_params=limit,
            cost_estimate=cost(one_conv if ring else RIM_FLOPS, 4 * 2**20),
            name="conv_one" if ring else "conv_one_rim",
        )(*args, vectors, *table_one, *more)

    hidden, stat_two = conv_one(True, ((2, rows, 0),))
    all_two = exchange(stat_two)
    rim, hidden_two = conv_one(False, ((0, 2, 0), (rows + 2, 2, 2)), hidden)
    hidden_before = lax.ppermute(hidden_two, "tm", down)
    w_up = pl.pallas_call(
        fold_kernel,
        out_shape=shape((2, 2, 2 * chan, chan), BF16),
        in_specs=[VM, HB],
        out_specs=VM,
        compiler_params=small,
        cost_estimate=cost(FILL_FLOPS, 2 * 2**20),
        name="fold",
    )(up_kernel.reshape(9, chan, chan // 2), stat_two)
    args_two = (own, hidden, rim, hidden_before, w_two, w_up)
    out_shape = shape((frames, 2 * rows, cols, chan), BF16)
    out = pl.pallas_call(
        conv_two_kernel,
        out_shape=out_shape,
        in_specs=[VM] * (len(args_two) + 3),
        out_specs=HB,
        scratch_shapes=[pltpu.VMEM(out_shape.shape, BF16)]
        + scratch(rows + 4)
        + [
            pltpu.VMEM((frames, rows + 2, cols, 128), BF16),
            pltpu.VMEM((frames, rows + 2, cols, 128), BF16),
            pltpu.SemaphoreType.DMA((frames,)),
        ],
        compiler_params=limit,
        cost_estimate=cost(3 * one_conv, 4 * 2**20),
        name="conv_two",
    )(*args_two, vectors, *table(all_two, gain_two))
    return out[None]


def solution(mesh):
    return jax.shard_map(
        body,
        mesh=mesh,
        in_specs=(P(None, "tm", "tile", None, None),) + (P(),) * 10,
        out_specs=P(None, "tm", "tile", None, None),
        check_vma=False,
    )
```
